256 devices in a mesh: ctx: 64 (over y, z, core), head: 4 (over x).
Axes of the slice: x: 4, y: 4, z: 8, core: 2. Of those that a mesh axis runs over, the one named last changes fastest.
Arguments:
- query_in: bfloat16 [8192, 4096], P('ctx', 'head'), may hold values from -6 to 6
- key_in: bfloat16 [8192, 4096], P('ctx', 'head'), may hold values from -6 to 6
- value_in: bfloat16 [8192, 4096], P('ctx', 'head')
- out_grad: bfloat16 [8192, 4096], P('ctx', 'head'), may hold values from -6 to 6
- chain_order: int32 [8192], P('ctx'), may hold values from 0 to 8191, as said below
- load_order: int32 [8192], P('ctx'), may hold values from 0 to 8191, as said below
- doc_lengths: int32 [128], replicated, may hold values from 1 to 2048, 8192 in all
Outputs:
- attended: bfloat16 [8192, 4096], P('ctx', 'head')
- query_grad: bfloat16 [8192, 4096], P('ctx', 'head')
- key_grad: bfloat16 [8192, 4096], P('ctx', 'head')
- value_grad: bfloat16 [8192, 4096], P('ctx', 'head')
The draws below stay inside these ranges and needn't reach their ends.
Inputs may be any that keep to these rules, and one draw needn't show every extreme that they name: `chain_order`: A permutation of the chain positions; load_order is its inverse. The number of tokens that ctx shard s loads and that belong to ctx shard d (chain positions d * 128 to d * 128 + 127) depends only on d - s modulo the number of shards; it is 1 to 4, and exactly 4 for one difference. `load_order`: the inverse of chain_order.
All inputs are finite; a program needn't handle non-finite values.
Results may differ from the reference program's by a relative error of at most 0.0059.
Values may be sent and summed in bfloat16 or wider, within the bound.
A program may use at most 192 MiB of HBM per device.

```python
import math
import jax
import jax.numpy as jnp
import numpy as np
from jax import lax

HEADS = 32
HEAD_DIM = 128
TOK_DEV = 128
FEATURES = 4096
TOKENS = 8192
CAP = 4
DOCS = 128
DOC_MOST = 2048


def order_pair(key):
    base_key = jax.random.fold_in(key, 7)
    key_weights, key_top, key_dest, key_source = jax.random.split(base_key, 4)
    shard_count = TOKENS // TOK_DEV
    others = shard_count - 1
    extra_rows = TOK_DEV - CAP - others
    weights = jax.random.randint(key_weights, (others,), 51, 101, dtype=jnp.int32)
    running = jnp.cumsum(weights).astype(jnp.int32)
    scaled_marks = extra_rows * running // running[-1]
    previous = jnp.concatenate([jnp.zeros((1,), jnp.int32), scaled_marks[:-1]])
    shares = 1 + scaled_marks - previous
    top_offset = jax.random.randint(key_top, (), 0, shard_count, dtype=jnp.int32)
    offsets = jnp.arange(shard_count, dtype=jnp.int32)
    picked = jnp.clip(offsets - (offsets > top_offset).astype(jnp.int32), 0, others - 1)
    counts_by_offset = jnp.where(offsets == top_offset, CAP, shares[picked]).astype(jnp.int32)
    bounds = jnp.cumsum(counts_by_offset).astype(jnp.int32)
    row_index = jnp.arange(TOK_DEV, dtype=jnp.int32)
    offset_of_row = jnp.sum((bounds[None, :] <= row_index[:, None]).astype(jnp.int32), axis=1)
    dest_perm = jax.vmap(lambda device: jax.random.permutation(jax.random.fold_in(key_dest, device), TOK_DEV))(offsets).astype(jnp.int32)
    source_perm = jax.vmap(lambda device: jax.random.permutation(jax.random.fold_in(key_source, device), TOK_DEV))(offsets).astype(jnp.int32)
    source_dev = (offsets[:, None] - offset_of_row[None, :]) % shard_count
    chain_pos = offsets[:, None] * TOK_DEV + dest_perm
    load_pos = source_dev * TOK_DEV + source_perm[source_dev, row_index[None, :]]
    flat_chain = chain_pos.reshape(-1)
    flat_load = load_pos.reshape(-1)
    load_order = jnp.zeros((TOKENS,), jnp.int32).at[flat_chain].set(flat_load)
    chain_order = jnp.zeros((TOKENS,), jnp.int32).at[flat_load].set(flat_chain)
    return (chain_order, load_order)


def draw_chain_order(key, part):
    return order_pair(key)[0]


def draw_load_order(key, part):
    return order_pair(key)[1]


def draw_value_in(key, part):
    key_spread, key_base = jax.random.split(key, 2)
    head_of = jnp.arange(FEATURES) // HEAD_DIM
    trend = 3.0 ** (head_of.astype(jnp.float32) / (HEADS - 1))
    spread = jnp.exp(jax.random.uniform(key_spread, (HEADS,), jnp.float32, 0.0, math.log(3.3)))
    base = jax.random.normal(key_base, (TOKENS, FEATURES), jnp.float32)
    return (base * (trend * spread[head_of])[None, :]).astype(jnp.bfloat16)


def steps_of(own_key, dims, shards, smallest, high):
    def one(dim, parts):
        steps = jax.random.uniform(jax.random.fold_in(jax.random.fold_in(own_key, 6), dim), (parts,), jnp.float32, smallest / len(shards), high / len(shards))
        return jnp.repeat(jnp.exp(steps), dims[dim] // parts).reshape((-1,) + (1,) * (len(dims) - dim - 1))

    factor_of = one(*shards[0])
    for cut in shards[1:]:
        factor_of = factor_of * one(*cut)
    return factor_of


def length_profile(number_of, total, reach, skew):
    portions = [(1 << 20) // math.isqrt(rank ** skew) + 1 for rank in range(2, number_of + 1)]
    spare, given = total - reach - (number_of - 1), [1] * (number_of - 1)
    while spare > 0:
        candidates = [i for i in range(number_of - 1) if given[i] < reach]
        whole, budget = sum([portions[i] for i in candidates]), spare
        for i in candidates:
            addition = min(reach - given[i], max(1, budget * portions[i] // whole), spare)
            given[i] = given[i] + addition
            spare = spare - addition
    return np.array([reach] + given)


def uneven_parts(stream_key, number_of, total, limit, skew):
    if number_of == 2:
        one = jax.random.randint(stream_key, (), max(1, total - limit), min(limit, total - 1) + 1)
        return jnp.stack([one, total - one])
    tallies = jnp.asarray(length_profile(number_of, total, limit, skew), jnp.int32)
    twos = (number_of - 1) // 2
    source_of, sink = tallies[1:1 + 2 * twos:2], tallies[2:2 + 2 * twos:2]
    room = jnp.minimum(source_of - 1, limit - sink)
    passed = jax.random.randint(jax.random.fold_in(stream_key, 1), (twos,), 0, 1 << 20) % (room + 1)
    tallies = tallies.at[1:1 + 2 * twos:2].set(source_of - passed).at[2:2 + 2 * twos:2].set(sink + passed)
    return tallies[jax.random.permutation(jax.random.fold_in(stream_key, 2), number_of)]


def centred(own_key, dims, scale, most, shards=(), kind=jnp.bfloat16):
    values = jax.random.normal(own_key, dims, jnp.float32) * scale
    if len(shards) > 0:
        values = steps_of(own_key, dims, shards, -0.22, 0.18) * values
    return jnp.clip(values, min=-most, max=most).astype(kind)


def setup_inputs(seed: int = 0) -> dict:
    streams_of = jax.random.split(jax.random.key(seed), 8)
    return {
        "query_in": centred(streams_of[0], (TOKENS, FEATURES), 1.0, 6.0, ((0, 64), (1, 4))),
        "key_in": centred(streams_of[1], (TOKENS, FEATURES), 1.0, 6.0, ((0, 64), (1, 4))),
        "value_in": draw_value_in(jax.random.fold_in(streams_of[7], 71), 0),
        "out_grad": centred(streams_of[3], (TOKENS, FEATURES), 1.0, 6.0, ((0, 64), (1, 4))),
        "chain_order": draw_chain_order(jax.random.fold_in(streams_of[7], 71), 0),
        "load_order": draw_load_order(jax.random.fold_in(streams_of[7], 71), 0),
        "doc_lengths": uneven_parts(streams_of[6], DOCS, TOKENS, DOC_MOST, 2).astype(jnp.int32),
    }


epsilon = 1e-06

def doc_index(positions, doc_ends):
    return lax.optimization_barrier(jnp.sum((doc_ends[None, :] <= positions[:, None]).astype(jnp.int32), axis=1))

def round_low(values):
    return lax.optimization_barrier(values.astype(jnp.bfloat16)).astype(jnp.float32)

def reference(query_in, key_in, value_in, out_grad, chain_order, load_order, doc_lengths):
    blocks = TOKENS // TOK_DEV
    highest = lax.Precision.HIGHEST

    def to_chain(source_array):
        return source_array[load_order].reshape(blocks, TOK_DEV, HEADS, HEAD_DIM)
    query_b = to_chain(query_in)
    key_b = to_chain(key_in)
    value_b = to_chain(value_in)
    grad_b = to_chain(out_grad)
    doc_ends = jnp.cumsum(doc_lengths).astype(jnp.int32)
    positions = jnp.arange(TOKENS, dtype=jnp.int32)
    docs_all = doc_index(positions, doc_ends).reshape(blocks, TOK_DEV)
    starts = jnp.arange(blocks, dtype=jnp.int32) * TOK_DEV
    prev_doc = doc_index(starts - 1, doc_ends)
    next_doc = doc_index(starts + TOK_DEV, doc_ends)
    carry_mask = (docs_all == prev_doc[:, None]).astype(jnp.float32)
    onward_mask = (docs_all == next_doc[:, None]).astype(jnp.float32)
    flags = (docs_all[:, -1] != prev_doc).astype(jnp.float32)
    local_index = jnp.arange(TOK_DEV, dtype=jnp.int32)
    causal = local_index[None, :] <= local_index[:, None]

    def block_within(docs):
        return (causal & (docs[:, None] == docs[None, :])).astype(jnp.float32)

    def block_scores(query_wide, key_wide, docs):
        scores = jnp.einsum('sha,tha->hst', query_wide, key_wide, precision=highest)
        return round_low(scores * block_within(docs)[None])

    def forward_step(state_in, inputs):
        query_blk, key_blk, value_blk, docs, carry_blk, onward_blk, flag = inputs
        query_wide = query_blk.astype(jnp.float32)
        key_wide = key_blk.astype(jnp.float32)
        value_wide = value_blk.astype(jnp.float32)
        state_low = round_low(state_in)
        attn_low = block_scores(query_wide, key_wide, docs)
        carried = jnp.einsum('sha,hab->shb', query_wide, state_low, precision=highest)
        raw_out = jnp.einsum('hst,thb->shb', attn_low, value_wide, precision=highest) + carry_blk[:, None, None] * carried
        summary = jnp.einsum('tha,thb->hab', key_wide, value_wide * onward_blk[:, None, None], precision=highest)
        new_state = summary + (1.0 - flag) * state_in
        return (new_state, (raw_out, state_in))
    start_state = jnp.zeros((HEADS, HEAD_DIM, HEAD_DIM), jnp.float32)
    unused_state, (raw_all, states) = lax.scan(forward_step, start_state, (query_b, key_b, value_b, docs_all, carry_mask, onward_mask, flags))
    squares = lax.optimization_barrier(jnp.sum(raw_all * raw_all, axis=(2, 3)))
    root_mean = jnp.sqrt(squares / FEATURES + epsilon)
    normed = raw_all / root_mean[:, :, None, None]
    attended_chain = normed.astype(jnp.bfloat16)
    grad_wide = grad_b.astype(jnp.float32)
    inner_mean = lax.optimization_barrier(jnp.sum(grad_wide * normed, axis=(2, 3))) / FEATURES
    dgrad = ((grad_wide - normed * inner_mean[:, :, None, None]) / root_mean[:, :, None, None]).astype(jnp.bfloat16)

    def backward_step(back_in, inputs):
        query_blk, key_blk, value_blk, dgrad_blk, docs, carry_blk, onward_blk, flag, state_in = inputs
        query_wide = query_blk.astype(jnp.float32)
        key_wide = key_blk.astype(jnp.float32)
        value_wide = value_blk.astype(jnp.float32)
        dgrad_wide = dgrad_blk.astype(jnp.float32)
        state_low = round_low(state_in)
        back_low = round_low(back_in)
        attn_low = block_scores(query_wide, key_wide, docs)
        mixed = jnp.einsum('shb,thb->hst', dgrad_wide, value_wide, precision=highest)
        mixed_low = round_low(mixed * block_within(docs)[None])
        query_out = jnp.einsum('hst,tha->sha', mixed_low, key_wide, precision=highest) + carry_blk[:, None, None] * jnp.einsum('shb,hab->sha', dgrad_wide, state_low, precision=highest)
        key_out = jnp.einsum('hst,sha->tha', mixed_low, query_wide, precision=highest) + onward_blk[:, None, None] * jnp.einsum('thb,hab->tha', value_wide, back_low, precision=highest)
        value_out = jnp.einsum('hst,shb->thb', attn_low, dgrad_wide, precision=highest) + onward_blk[:, None, None] * jnp.einsum('tha,hab->thb', key_wide, back_low, precision=highest)
        summary = jnp.einsum('tha,thb->hab', query_wide, dgrad_wide * carry_blk[:, None, None], precision=highest)
        new_back = summary + (1.0 - flag) * back_in
        outputs = (query_out.astype(jnp.bfloat16), key_out.astype(jnp.bfloat16), value_out.astype(jnp.bfloat16))
        return (new_back, outputs)
    unused_back, (query_chain, key_chain, value_chain) = lax.scan(backward_step, start_state, (query_b, key_b, value_b, dgrad, docs_all, carry_mask, onward_mask, flags, states), reverse=True)

    def to_load(chain_array):
        return chain_array.reshape(TOKENS, FEATURES)[chain_order]
    return (to_load(attended_chain), to_load(query_chain), to_load(key_chain), to_load(value_chain))
```

```python
import functools
import jax
import jax.numpy as jnp
from jax import lax
from jax.experimental import pallas as pl
from jax.experimental.pallas import tpu as pltpu
from jax.sharding import PartitionSpec as P

HEAD_DIM = 128
FEATURES = 4096


epsilon = 1e-06


def carried_in(value, axis, join, neutral, backward):
    count, mine = (lax.axis_size(axis), lax.axis_index(axis))
    pieces = jax.tree.map(lambda part: lax.all_gather(part, axis), value)
    if backward:
        pieces = jax.tree.map(lambda part: part[::-1], pieces)
        mine = count - 1 - mine
    subtotal = jax.tree.map(
        lambda part, zero: jnp.full_like(part, 0) + jnp.asarray(zero, part.dtype), value, neutral
    )

    def step(position, subtotal):
        longer = join(subtotal, jax.tree.map(lambda part: part[position], pieces))
        return jax.tree.map(lambda new, old: jnp.where(position < mine, new, old), longer, subtotal)

    return lax.fori_loop(0, count - 1, step, subtotal)


def rank_within(groups, values):
    same_group = groups[:, None] == groups[None, :]
    before = values[None, :] < values[:, None]
    return jnp.sum((same_group & before).astype(jnp.int32), axis=1)


def pack_rows(rows_in, slot_index, slot_total):
    return jnp.zeros((slot_total, rows_in.shape[1]), rows_in.dtype).at[slot_index].set(rows_in)


def doc_index(positions, doc_ends):
    return jnp.sum((doc_ends[None, :] <= positions[:, None]).astype(jnp.int32), axis=1)


def chain_combine(earlier, later_one):
    return (later_one[0] + (1.0 - later_one[1]) * earlier[0], jnp.maximum(earlier[1], later_one[1]))


def general_body(query_in, key_in, value_in, out_grad, chain_order, load_order, doc_lengths):
    row_count, width_dev = query_in.shape
    heads_dev = width_dev // HEAD_DIM
    shards = lax.axis_size("ctx")
    capacity = 2 * row_count // shards
    slot_total = shards * capacity
    local_index = jnp.arange(row_count, dtype=jnp.int32)
    dest_dev = chain_order // row_count
    send_slot = dest_dev * capacity + rank_within(dest_dev, local_index)
    source_dev = load_order // row_count
    recv_slot = source_dev * capacity + rank_within(source_dev, load_order)

    def arrive(packed):
        return packed[recv_slot]

    def depart(packed):
        return packed[send_slot]

    arrived = (
        lax.all_to_all(
            pack_rows(query_in, send_slot, slot_total),
            "ctx",
            split_axis=0,
            concat_axis=0,
            tiled=True,
        ),
        lax.all_to_all(
            pack_rows(key_in, send_slot, slot_total), "ctx", split_axis=0, concat_axis=0, tiled=True
        ),
        lax.all_to_all(
            pack_rows(value_in, send_slot, slot_total),
            "ctx",
            split_axis=0,
            concat_axis=0,
            tiled=True,
        ),
        lax.all_to_all(
            pack_rows(out_grad, send_slot, slot_total),
            "ctx",
            split_axis=0,
            concat_axis=0,
            tiled=True,
        ),
    )
    query_rows, key_rows, value_rows, grad_rows = jax.tree.map(arrive, arrived)
    query_heads = query_rows.reshape(row_count, heads_dev, HEAD_DIM)
    key_heads = key_rows.reshape(row_count, heads_dev, HEAD_DIM)
    value_heads = value_rows.reshape(row_count, heads_dev, HEAD_DIM)
    doc_ends = jnp.cumsum(doc_lengths)
    first_row = lax.axis_index("ctx") * row_count
    docs_here = doc_index(first_row + local_index, doc_ends)
    border = doc_index(first_row + jnp.array([-1, row_count], jnp.int32), doc_ends)
    carry_in = (docs_here == border[0]).astype(jnp.float32)
    onward = docs_here == border[1]
    onward_wide = onward.astype(jnp.float32)
    has_start = (docs_here[-1] != border[0]).astype(jnp.float32)
    causal = local_index[None, :] <= local_index[:, None]
    within = (causal & (docs_here[:, None] == docs_here[None, :])).astype(jnp.float32)
    kept_values = jnp.where(onward[:, None, None], value_heads, jnp.zeros_like(value_heads))
    forward_part = jnp.einsum(
        "tha,thb->hab", key_heads, kept_values, preferred_element_type=jnp.float32
    )
    identity = (jnp.zeros_like(forward_part), jnp.zeros((), jnp.float32))
    state_in, unused_flag = carried_in(
        (forward_part, has_start), "ctx", chain_combine, identity, False
    )
    scores = jnp.einsum("sha,tha->hst", query_heads, key_heads, preferred_element_type=jnp.float32)
    attn_low = (scores * within[None]).astype(jnp.bfloat16)
    state_low = state_in.astype(jnp.bfloat16)
    carried = jnp.einsum("sha,hab->shb", query_heads, state_low, preferred_element_type=jnp.float32)
    raw_out = (
        jnp.einsum("hst,thb->shb", attn_low, value_heads, preferred_element_type=jnp.float32)
        + carry_in[:, None, None] * carried
    )
    squares = jnp.sum(raw_out * raw_out, axis=(1, 2))
    grad_wide = grad_rows.reshape(row_count, heads_dev, HEAD_DIM).astype(jnp.float32)
    total_sq = lax.psum(squares, "head")
    root_mean = jnp.sqrt(total_sq / FEATURES + epsilon)
    normed = raw_out / root_mean[:, None, None]
    inner_mean = lax.psum(jnp.sum(grad_wide * normed, axis=(1, 2)), "head") / FEATURES
    attended_rows = normed.astype(jnp.bfloat16).reshape(row_count, width_dev)
    dgrad = ((grad_wide - normed * inner_mean[:, None, None]) / root_mean[:, None, None]).astype(
        jnp.bfloat16
    )
    kept_grad = jnp.where(carry_in[:, None, None] > 0, dgrad, jnp.zeros_like(dgrad))
    reverse_part = jnp.einsum(
        "tha,thb->hab", query_heads, kept_grad, preferred_element_type=jnp.float32
    )
    reverse_in, unused_back = carried_in(
        (reverse_part, has_start), "ctx", chain_combine, identity, True
    )
    mixed = jnp.einsum("shb,thb->hst", dgrad, value_heads, preferred_element_type=jnp.float32)
    mixed_low = (mixed * within[None]).astype(jnp.bfloat16)
    query_out = jnp.einsum(
        "hst,tha->sha", mixed_low, key_heads, preferred_element_type=jnp.float32
    ) + carry_in[:, None, None] * jnp.einsum(
        "shb,hab->sha", dgrad, state_low, preferred_element_type=jnp.float32
    )
    reverse_low = reverse_in.astype(jnp.bfloat16)
    key_out = jnp.einsum(
        "hst,sha->tha", mixed_low, query_heads, preferred_element_type=jnp.float32
    ) + onward_wide[:, None, None] * jnp.einsum(
        "thb,hab->tha", value_heads, reverse_low, preferred_element_type=jnp.float32
    )
    value_out = jnp.einsum(
        "hst,shb->thb", attn_low, dgrad, preferred_element_type=jnp.float32
    ) + onward_wide[:, None, None] * jnp.einsum(
        "tha,hab->thb", key_heads, reverse_low, preferred_element_type=jnp.float32
    )
    query_low = query_out.astype(jnp.bfloat16).reshape(row_count, width_dev)
    key_low = key_out.astype(jnp.bfloat16).reshape(row_count, width_dev)
    value_low = value_out.astype(jnp.bfloat16).reshape(row_count, width_dev)
    returned = (
        lax.all_to_all(
            pack_rows(attended_rows, recv_slot, slot_total),
            "ctx",
            split_axis=0,
            concat_axis=0,
            tiled=True,
        ),
        lax.all_to_all(
            pack_rows(query_low, recv_slot, slot_total),
            "ctx",
            split_axis=0,
            concat_axis=0,
            tiled=True,
        ),
        lax.all_to_all(
            pack_rows(key_low, recv_slot, slot_total),
            "ctx",
            split_axis=0,
            concat_axis=0,
            tiled=True,
        ),
        lax.all_to_all(
            pack_rows(value_low, recv_slot, slot_total),
            "ctx",
            split_axis=0,
            concat_axis=0,
            tiled=True,
        ),
    )
    attended, query_grad, key_grad, value_grad = jax.tree.map(depart, returned)
    return (attended, query_grad, key_grad, value_grad)


SOURCES = 64
GROUPS = 8
MAIN = 16
EXTRA = 4
ROWS = 4 * (MAIN + EXTRA)
MAIN_SLOTS = SOURCES * MAIN
SLOTS = SOURCES * (MAIN + EXTRA)
GROUP_TOKENS = 1024
TILE = 128
PART = 256
TILES = SLOTS // TILE
PARTS = SLOTS // PART
TOKENS = 8192
HEADS_HERE = 8
MESH = pl.DeviceIdType.MESH
F32 = jnp.float32
LOW = jnp.bfloat16


def nn(left, right, precision=None):
    return lax.dot_general(
        left, right, (((1,), (0,)), ((), ())), precision=precision, preferred_element_type=F32
    )


def nt(left, right, precision=None):
    return lax.dot_general(
        left, right, (((1,), (1,)), ((), ())), precision=precision, preferred_element_type=F32
    )


def tn(left, right):
    return lax.dot_general(left, right, (((0,), (0,)), ((), ())), preferred_element_type=F32)


def iota(shape, dim):
    return lax.broadcasted_iota(jnp.int32, shape, dim)


def turned(row):
    return jnp.transpose(jnp.broadcast_to(row, (TILE, TILE)))


def ones_where(mask):
    return jnp.where(mask, 1.0, 0.0)


def group_and_rank(chain_row, axis):
    across = jnp.broadcast_to(chain_row, (TILE, TILE))
    down = jnp.transpose(across)
    group_across = jnp.floor(across * (1.0 / GROUP_TOKENS))
    group_down = jnp.floor(down * (1.0 / GROUP_TOKENS))
    same = group_across == group_down
    if axis == 0:
        rank = jnp.sum(ones_where(same & (down < across)), axis=0, keepdims=True)
        return group_across[0:1], rank
    rank = jnp.sum(ones_where(same & (across < down)), axis=1, keepdims=True)
    return group_down[:, 0:1], rank


def fused_kernel(
    query_hbm,
    key_hbm,
    value_hbm,
    grad_hbm,
    chain_ref,
    load_ref,
    length_ref,
    back_ref,
    rows_in,
    packed,
    landed,
    outgoing,
    load_own,
    load_all,
    spread,
    gathered,
    pos_wide,
    start_wide,
    carry_wide,
    onward_wide,
    root_wide,
    inner_wide,
    row_facts,
    queries,
    keys,
    values,
    grads,
    dgrads,
    raw,
    key_sum,
    value_sum,
    extra_out,
    scores_turned,
    state_own,
    state_all,
    back_own,
    back_all,
    stage_one,
    stage_two,
    in_sem,
    load_sem,
    data_send,
    data_recv,
    state_send,
    state_recv,
    sum_send,
    sum_recv,
    out_send,
    out_recv,
):
    place, x = lax.axis_index("ctx"), lax.axis_index("head")
    y, z, c = place // 16, lax.rem(place // 2, 8), lax.rem(place, 2)
    mine = y * 2 + c

    def at(j, zz):
        yy, cc = lax.rem(y + j // 2, 4), lax.rem(c + lax.rem(j, 2), 2)
        return (yy * 8 + zz) * 2 + cc, yy * 2 + cc

    def remote(src, dst, send, recv, ctx, head):
        return pltpu.make_async_remote_copy(
            src_ref=src,
            dst_ref=dst,
            send_sem=send,
            recv_sem=recv,
            device_id=(ctx, head),
            device_id_type=MESH,
        )

    def settle(ref, sem):
        pltpu.make_async_copy(ref, ref, sem).wait()

    inputs = (query_hbm, key_hbm, value_hbm, grad_hbm)
    for a, source in enumerate(inputs):
        pltpu.make_async_copy(source, rows_in.at[pl.ds(a * TILE, TILE)], in_sem.at[a]).start()

    barrier = pltpu.get_barrier_semaphore()

    def greet(i, carry):
        ctx, unused = at(lax.rem(i, 8), lax.rem(z + i // 8, 8))
        pl.semaphore_signal(barrier, inc=1, device_id=(ctx, x), device_id_type=MESH)
        return carry

    lax.fori_loop(1, 64, greet, 0)
    for j in range(1, 4):
        pl.semaphore_signal(
            barrier, inc=1, device_id=(place, lax.rem(x + j, 4)), device_id_type=MESH
        )

    group, rank = group_and_rank(chain_ref[...].astype(F32), 0)
    targets = []
    for a in range(4):
        main_row = (a * MAIN if a < 3 else 3 * MAIN + 4 * EXTRA) + rank
        extra_row = 3 * MAIN + a * EXTRA + rank - MAIN
        targets.append(group * ROWS + jnp.where(rank < MAIN, main_row, extra_row))
    target = jnp.concatenate(targets, axis=1).astype(jnp.int32)
    load_own[...] = jnp.broadcast_to(load_ref[...], (8, TILE))
    for a, source in enumerate(inputs):
        pltpu.make_async_copy(source, rows_in.at[pl.ds(a * TILE, TILE)], in_sem.at[a]).wait()
    pl.semaphore_wait(barrier, 66)

    owner = place // 8
    for j in range(8):
        ctx, unused = at(j, owner)
        send = load_sem.at[1 if j == 0 else 0]
        if j == 0:

            @pl.when(owner == z)
            def _():
                pltpu.make_async_copy(
                    load_own, load_all.at[lax.rem(place, 8)], load_sem.at[2]
                ).start()

            @pl.when(owner != z)
            def _():
                remote(
                    load_own, load_all.at[lax.rem(place, 8)], send, load_sem.at[2], ctx, x
                ).start()
        else:
            remote(load_own, load_all.at[lax.rem(place, 8)], send, load_sem.at[2], ctx, x).start()

    early, late = pl.ds(0, 64), pl.ds(64, 16)
    row_number = iota((ROWS, 4 * TILE), 0)

    def send_rows(slot, ctx, rows, recv):
        remote(
            packed.at[slot, rows], landed.at[place, rows], data_send, data_recv.at[recv], ctx, x
        ).start()

    def keep_rows(slot, rows, recv):
        pltpu.make_async_copy(
            packed.at[slot, rows], landed.at[place, rows], data_recv.at[recv]
        ).start()

    def pack_group(i, carry):
        goal = lax.rem(z + i + 1, 8)
        pick = ones_where(row_number + goal * ROWS == target).astype(LOW)
        block = nn(pick, rows_in[...]).astype(LOW)
        for head in range(HEADS_HERE):
            packed[goal * 8 + head] = block[:, head * TILE : (head + 1) * TILE]
        for j in range(8):
            ctx, head = at(j, goal)
            if j == 0:

                @pl.when(i < 7)
                def _():
                    send_rows(goal * 8 + head, ctx, early, 0)

            else:
                send_rows(goal * 8 + head, ctx, early, 0)
        return carry

    lax.fori_loop(0, 8, pack_group, 0)
    keep_rows(z * 8 + mine, early, 0)
    keep_rows(z * 8 + mine, late, 1)

    def send_late(i, carry):
        goal = lax.rem(z + i // 8, 8)
        ctx, head = at(lax.rem(i, 8), goal)
        send_rows(goal * 8 + head, ctx, late, 1)
        return carry

    lax.fori_loop(1, 64, send_late, 0)

    down, across = iota((TILE, TILE), 0), iota((TILE, TILE), 1)
    lengths = jnp.broadcast_to(length_ref[...].astype(F32), (TILE, TILE))
    ends_down = jnp.sum(jnp.where(across <= down, lengths, 0.0), axis=1, keepdims=True)
    ends = jnp.transpose(jnp.broadcast_to(ends_down, (TILE, TILE)))
    base = (z * GROUP_TOKENS).astype(F32)
    top = base + float(GROUP_TOKENS)

    def goes_on(last_tokens, first):
        start = jnp.max(
            jnp.where(ends[0:1] <= last_tokens - 1.0, ends[0:1], 0.0), axis=1, keepdims=True
        )
        return ones_where(start < first)

    def spreading(shape, first):
        number, other = iota(shape, first), iota(shape, 1 - first)
        array, rest = number // 256, lax.rem(number, 256)
        goal = (rest // 4) * 16 + array * 4 + lax.rem(rest, 4)
        return ones_where(goal == other).astype(LOW)

    def fill_spread(i, carry):
        number = iota((TILE, 1024), 0) + i * TILE
        array, rest = number // 256, lax.rem(number, 256)
        goal = (rest // 4) * 16 + array * 4 + lax.rem(rest, 4)
        rows = pl.ds(pl.multiple_of(i * TILE, TILE), TILE)
        gathered[rows] = ones_where(goal == iota((TILE, 1024), 1)).astype(LOW)
        source, rest = number // 16, lax.rem(number, 16)
        origin = (rest // 4) * 256 + source * 4 + lax.rem(rest, 4)
        spread[rows] = ones_where(origin == iota((TILE, 1024), 1)).astype(LOW)
        return carry

    lax.fori_loop(0, 8, fill_spread, 0)

    settle(load_all, load_sem.at[2])
    below = ones_where(across < down).astype(LOW)
    slot_number = iota((TILE, SLOTS), 1).astype(F32)
    fact_row, fact_lane = iota((8, TILE), 0), iota((8, TILE), 1)
    seen = jnp.zeros((1, TILE), F32)
    facts = jnp.zeros((8, SLOTS), F32)
    for j in range(8):
        source = (load_all[j, 0:1] // TILE).astype(F32)
        source_wide = turned(source)
        same = ones_where(source_wide == across.astype(F32))
        earlier = nn(below, same.astype(LOW)) + seen
        place_in = jnp.sum(same * earlier, axis=1, keepdims=True)
        seen = seen + jnp.sum(same, axis=0, keepdims=True)
        source_column = source_wide[:, 0:1]
        slot = jnp.where(
            place_in < MAIN,
            source_column * MAIN + place_in,
            MAIN_SLOTS + source_column * EXTRA + place_in - MAIN,
        )
        pick = ones_where(slot == slot_number).astype(LOW)
        told = jnp.where(
            fact_row == 0, j, jnp.where(fact_row == 1, fact_lane, jnp.where(fact_row == 2, 1, 0))
        )
        facts = facts + nn(told.astype(F32).astype(LOW), pick)
    position = jnp.where(facts[2:3] > 0.5, base + facts[0:1] * TILE + facts[1:2], -1.0)
    row_facts[0:1] = position
    for t in range(TILES):
        tile = slice(t * TILE, (t + 1) * TILE)
        where = turned(position[:, tile])
        start = jnp.max(jnp.where(ends <= where, ends, 0.0), axis=1, keepdims=True)
        end = jnp.min(jnp.where(ends > where, ends, float(TOKENS)), axis=1, keepdims=True)
        start_all = jnp.broadcast_to(start, (TILE, TILE))
        pos_wide[tile] = where
        start_wide[tile] = start_all
        carry_wide[tile] = ones_where((start_all < base) & (where >= 0.0))
        onward_wide[tile] = ones_where((jnp.broadcast_to(end, (TILE, TILE)) > top) & (where >= 0.0))
        row_facts[1:2, tile] = jnp.transpose(start_all)[0:1]

    def part(i):
        return pl.ds(pl.multiple_of(i * PART, PART), PART)

    settle(landed.at[:, early], data_recv.at[0])
    extra = nn(gathered[...], landed[:, 48:64].reshape(1024, TILE)).astype(LOW)
    for a, ref in enumerate((queries, keys, values)):
        ref[0:MAIN_SLOTS] = landed[:, a * MAIN : (a + 1) * MAIN].reshape(MAIN_SLOTS, TILE)
        ref[MAIN_SLOTS:SLOTS] = extra[a * 256 : (a + 1) * 256]
    grads[MAIN_SLOTS:SLOTS] = extra[768:1024]

    kept = (keys[...].astype(F32) * onward_wide[...]).astype(LOW)
    state_own[...] = tn(kept, values[...])
    for n in (1, 2):
        ctx, unused = at(0, lax.rem(z + n, 8))
        remote(
            state_own, state_all.at[n - 1], state_send.at[0], state_recv.at[n - 1], ctx, x
        ).start()

    def forward_part(i, carry):
        rows = part(i)
        where, start = pos_wide[rows][:, 0:1], start_wide[rows][:, 0:1]
        inside = (row_facts[0:1] <= where) & (row_facts[0:1] >= start)
        scores = nt(queries[rows], keys[...])
        low = jnp.where(inside, scores, 0.0).astype(LOW)
        raw[rows] = nn(low, values[...])
        return carry

    lax.fori_loop(0, PARTS, forward_part, 0)
    settle(state_all.at[0], state_recv.at[0])
    settle(state_all.at[1], state_recv.at[1])
    state = state_all[0] + goes_on(base, base - float(GROUP_TOKENS)) * state_all[1]
    state_low = state.astype(LOW)
    raw[...] = raw[...] + carry_wide[...] * nn(queries[...], state_low)

    def tile_sums(product):
        row = iota((16, TILE), 0)
        total = jnp.zeros((16, TILE), F32)
        ones = jnp.ones((16, TILE), F32)
        for t in range(TILES):
            tile = product(slice(t * TILE, (t + 1) * TILE))
            total = jnp.where(row == t, nt(ones, tile, lax.Precision.HIGHEST), total)
        return total

    def head_sum_start(k, partial):
        stage_one[k, mine] = partial
        for j in range(1, 8):
            ctx, unused = at(j, z)
            remote(
                stage_one.at[k, mine],
                stage_one.at[k, mine],
                sum_send.at[2 * k],
                sum_recv.at[2 * k],
                ctx,
                x,
            ).start()

    def head_sum_next(k):
        settle(stage_one.at[k, pl.ds(0, 7)], sum_recv.at[2 * k])
        total = stage_one[k, 0]
        for j in range(1, 8):
            total = total + stage_one[k, j]
        stage_two[k, x] = total
        for j in range(1, 4):
            remote(
                stage_two.at[k, x],
                stage_two.at[k, x],
                sum_send.at[2 * k + 1],
                sum_recv.at[2 * k + 1],
                place,
                lax.rem(x + j, 4),
            ).start()

    def head_sum_end(k):
        settle(stage_two.at[k, pl.ds(0, 3)], sum_recv.at[2 * k + 1])
        return (stage_two[k, 0] + stage_two[k, 1]) + (stage_two[k, 2] + stage_two[k, 3])

    head_sum_start(0, tile_sums(lambda tile: raw[tile] * raw[tile]))

    def turned_part(i, carry):
        rows = part(i)
        where = pos_wide[rows][:, 0:1]
        inside = (where <= row_facts[0:1]) & (where >= row_facts[1:2])
        scores = nt(keys[rows], queries[...])
        scores_turned[rows] = jnp.where(inside, scores, 0.0).astype(LOW)
        return carry

    lax.fori_loop(0, PARTS, turned_part, 0)
    head_sum_next(0)
    settle(landed.at[:, late], data_recv.at[1])
    grads[0:MAIN_SLOTS] = landed[:, 64:80].reshape(MAIN_SLOTS, TILE)
    head_sum_start(1, tile_sums(lambda tile: raw[tile] * grads[tile].astype(F32)))
    total = head_sum_end(0)
    inverse = 1.0 / jnp.sqrt(total / FEATURES + epsilon)
    for t in range(TILES):
        root_wide[t * TILE : (t + 1) * TILE] = turned(inverse[t : t + 1])
    raw[...] = raw[...] * root_wide[...]
    attended = raw[...].astype(LOW)
    outgoing[:, 0:MAIN] = attended[0:MAIN_SLOTS].reshape(SOURCES, MAIN, TILE)
    extra_out[0:256] = attended[MAIN_SLOTS:SLOTS]
    head_sum_next(1)

    def send_back(rows):
        def one(i, carry):
            ctx, unused = at(lax.rem(i, 8), lax.rem(z + i // 8, 8))
            remote(
                outgoing.at[ctx, rows], back_ref.at[z, mine, rows], out_send, out_recv, ctx, x
            ).start()
            return carry

        lax.fori_loop(1, 64, one, 0)
        pltpu.make_async_copy(
            outgoing.at[place, rows], back_ref.at[z, mine, rows], out_recv
        ).start()

    send_back(pl.ds(0, MAIN))
    inner = head_sum_end(1) * inverse / FEATURES
    for t in range(TILES):
        inner_wide[t * TILE : (t + 1) * TILE] = turned(inner[t : t + 1])
    dgrads[...] = (
        (grads[...].astype(F32) - raw[...] * inner_wide[...]) * root_wide[...]
    ).astype(LOW)

    kept_queries = (queries[...].astype(F32) * carry_wide[...]).astype(LOW)
    back_own[...] = tn(kept_queries, dgrads[...])
    for n in (1, 2):
        ctx, unused = at(0, lax.rem(z + 8 - n, 8))
        remote(
            back_own, back_all.at[n - 1], state_send.at[1], state_recv.at[n + 1], ctx, x
        ).start()

    for i in range(PARTS):
        rows = slice(i * PART, (i + 1) * PART)
        where, start = pos_wide[rows, 0:1], start_wide[rows, 0:1]
        inside = (row_facts[0:1] <= where) & (row_facts[0:1] >= start)
        mixed = jnp.where(inside, nt(dgrads[rows], values[...]), 0.0).astype(LOW)
        query_part = nn(mixed, keys[...]) + carry_wide[rows] * nt(dgrads[rows], state_low)
        query_low = query_part.astype(LOW)
        if i < MAIN_SLOTS // PART:
            outgoing[i * 16 : (i + 1) * 16, MAIN : 2 * MAIN] = query_low.reshape(16, MAIN, TILE)
        else:
            extra_out[256:512] = query_low
    send_back(pl.ds(MAIN, MAIN))

    def key_value_part(i, carry):
        rows = part(i)
        where = pos_wide[rows][:, 0:1]
        inside = (where <= row_facts[0:1]) & (where >= row_facts[1:2])
        mixed = jnp.where(inside, nt(values[rows], dgrads[...]), 0.0).astype(LOW)
        key_sum[rows] = nn(mixed, queries[...])
        value_sum[rows] = nn(scores_turned[rows], dgrads[...])
        return carry

    lax.fori_loop(0, PARTS, key_value_part, 0)
    settle(back_all.at[0], state_recv.at[2])
    settle(back_all.at[1], state_recv.at[3])
    back = back_all[0] + goes_on(top + float(GROUP_TOKENS), top) * back_all[1]
    back_low = back.astype(LOW)
    key_low = (key_sum[...] + onward_wide[...] * nt(values[...], back_low)).astype(LOW)
    value_low = (value_sum[...] + onward_wide[...] * nn(keys[...], back_low)).astype(LOW)
    outgoing[:, 2 * MAIN : 3 * MAIN] = key_low[0:MAIN_SLOTS].reshape(SOURCES, MAIN, TILE)
    outgoing[:, 3 * MAIN : 4 * MAIN] = value_low[0:MAIN_SLOTS].reshape(SOURCES, MAIN, TILE)
    extra_out[512:768] = key_low[MAIN_SLOTS:SLOTS]
    extra_out[768:1024] = value_low[MAIN_SLOTS:SLOTS]
    extra_rows = nn(spread[...], extra_out[...]).astype(LOW)
    outgoing[:, 4 * MAIN : ROWS] = extra_rows.reshape(SOURCES, 4 * EXTRA, TILE)
    send_back(pl.ds(2 * MAIN, 3 * MAIN))

    settle(load_all.at[pl.ds(0, 7)], load_sem.at[0])

    @pl.when(owner != z)
    def _():
        settle(load_own, load_sem.at[1])

    settle(packed.at[pl.ds(0, 63)], data_send)
    settle(state_all, state_send.at[0])
    settle(back_all, state_send.at[1])
    for k in range(2):
        settle(stage_one.at[k, pl.ds(0, 7)], sum_send.at[2 * k])
        settle(stage_two.at[k, pl.ds(0, 3)], sum_send.at[2 * k + 1])
    settle(outgoing.at[pl.ds(0, 63)], out_send)
    settle(outgoing, out_recv)


def unpack_kernel(chain_ref, back_ref, attended_ref, query_ref, key_ref, value_ref):
    group, rank = group_and_rank(chain_ref[...].astype(F32), 1)
    number = iota((TILE, GROUPS * ROWS), 1).astype(F32)
    picks = []
    for a in range(4):
        row = jnp.where(rank < MAIN, a * MAIN + rank, 4 * MAIN + a * EXTRA + rank - MAIN)
        picks.append(ones_where(group * ROWS + row == number).astype(LOW))
    pick = jnp.concatenate(picks, axis=0)
    for head in range(HEADS_HERE):
        found = nn(pick, back_ref[:, head].reshape(GROUPS * ROWS, TILE)).astype(LOW)
        lanes = slice(head * TILE, (head + 1) * TILE)
        for a, ref in enumerate((attended_ref, query_ref, key_ref, value_ref)):
            ref[:, lanes] = found[a * TILE : (a + 1) * TILE]


def fast_body(query_in, key_in, value_in, out_grad, chain_order, load_order, doc_lengths):
    chain_row = chain_order.reshape(1, TILE)
    whole = pl.BlockSpec(memory_space=pltpu.VMEM)
    anywhere = pl.BlockSpec(memory_space=pl.ANY)
    wide = pltpu.VMEM((SLOTS, TILE), F32)
    low = pltpu.VMEM((SLOTS, TILE), LOW)
    dma = pltpu.SemaphoreType.DMA
    returned = pl.pallas_call(
        fused_kernel,
        out_shape=jax.ShapeDtypeStruct((GROUPS, HEADS_HERE, ROWS, TILE), LOW),
        in_specs=[anywhere] * 4 + [whole] * 3,
        out_specs=anywhere,
        scratch_shapes=[
            pltpu.VMEM((4 * TILE, HEADS_HERE * TILE), LOW),
            pltpu.VMEM((SOURCES, ROWS, TILE), LOW),
            pltpu.VMEM((SOURCES, ROWS, TILE), LOW),
            pltpu.VMEM((SOURCES, ROWS, TILE), LOW),
            pltpu.VMEM((8, TILE), jnp.int32),
            pltpu.VMEM((8, 8, TILE), jnp.int32),
            pltpu.VMEM((1024, 1024), LOW),
            pltpu.VMEM((1024, 1024), LOW),
            wide,
            wide,
            wide,
            wide,
            wide,
            wide,
            pltpu.VMEM((8, SLOTS), F32),
            low,
            low,
            low,
            low,
            low,
            wide,
            wide,
            wide,
            pltpu.VMEM((1024, TILE), LOW),
            pltpu.VMEM((SLOTS, SLOTS), LOW),
            pltpu.VMEM((TILE, TILE), F32),
            pltpu.VMEM((2, TILE, TILE), F32),
            pltpu.VMEM((TILE, TILE), F32),
            pltpu.VMEM((2, TILE, TILE), F32),
            pltpu.VMEM((2, 8, 16, TILE), F32),
            pltpu.VMEM((2, 4, 16, TILE), F32),
            dma((4,)),
            dma((3,)),
            dma,
            dma((2,)),
            dma((2,)),
            dma((4,)),
            dma((4,)),
            dma((4,)),
            dma,
            dma,
        ],
        compiler_params=pltpu.CompilerParams(
            collective_id=0, has_side_effects=True, vmem_limit_bytes=48 << 20
        ),
        name="fused",
    )(
        query_in,
        key_in,
        value_in,
        out_grad,
        chain_row,
        load_order.reshape(1, TILE),
        doc_lengths.reshape(1, TILE),
    )
    out = jax.ShapeDtypeStruct((TILE, HEADS_HERE * TILE), LOW)
    return pl.pallas_call(
        unpack_kernel,
        out_shape=(out,) * 4,
        in_specs=[whole] * 2,
        out_specs=(whole,) * 4,
        compiler_params=pltpu.CompilerParams(vmem_limit_bytes=32 << 20),
        name="unpack",
    )(chain_row, returned)


def body(query_in, key_in, value_in, out_grad, chain_order, load_order, doc_lengths):
    ahead = jnp.mod(chain_order // TILE - lax.axis_index("ctx"), SOURCES)
    windows = jnp.mod(ahead[None, :] - jnp.arange(SOURCES)[:, None], SOURCES) < GROUPS
    most = jnp.max(jnp.sum(windows.astype(jnp.int32), axis=1))
    return lax.cond(
        most <= MAIN + EXTRA,
        fast_body,
        general_body,
        query_in,
        key_in,
        value_in,
        out_grad,
        chain_order,
        load_order,
        doc_lengths,
    )


def solution(mesh):
    return jax.shard_map(
        body,
        mesh=mesh,
        in_specs=(
            P("ctx", "head"),
            P("ctx", "head"),
            P("ctx", "head"),
            P("ctx", "head"),
            P("ctx"),
            P("ctx"),
            P(),
        ),
        out_specs=(P("ctx", "head"), P("ctx", "head"), P("ctx", "head"), P("ctx", "head")),
        check_vma=False,
    )
```

```python
import functools
import jax
import jax.numpy as jnp
from jax import lax
from jax.experimental import pallas as pl
from jax.experimental.pallas import tpu as pltpu
from jax.sharding import PartitionSpec as P

HEAD_DIM = 128
FEATURES = 4096

epsilon = 1e-06

SOURCES = 64
GROUPS = 8
GROUP_TOKENS = 1024
TILE = 128
PART = 256
TOKENS = 8192
HEADS_HERE = 8
SMALL = (16, 4)
LARGE = (32, 0)
MESH = pl.DeviceIdType.MESH
F32 = jnp.float32
LOW = jnp.bfloat16


def nn(left, right, precision=None):
    return lax.dot_general(
        left, right, (((1,), (0,)), ((), ())), precision=precision, preferred_element_type=F32
    )


def nt(left, right, precision=None):
    return lax.dot_general(
        left, right, (((1,), (1,)), ((), ())), precision=precision, preferred_element_type=F32
    )


def tn(left, right):
    return lax.dot_general(left, right, (((0,), (0,)), ((), ())), preferred_element_type=F32)


def iota(shape, dim):
    return lax.broadcasted_iota(jnp.int32, shape, dim)


def turned(row):
    return jnp.transpose(jnp.broadcast_to(row, (TILE, TILE)))


def ones_where(mask):
    return jnp.where(mask, 1.0, 0.0)


def group_and_rank(chain_row, axis):
    across = jnp.broadcast_to(chain_row, (TILE, TILE))
    down = jnp.transpose(across)
    group_across = jnp.floor(across * (1.0 / GROUP_TOKENS))
    group_down = jnp.floor(down * (1.0 / GROUP_TOKENS))
    same = group_across == group_down
    if axis == 0:
        rank = jnp.sum(ones_where(same & (down < across)), axis=0, keepdims=True)
        return group_across[0:1], rank
    rank = jnp.sum(ones_where(same & (across < down)), axis=1, keepdims=True)
    return group_down[:, 0:1], rank


def fused_kernel(
    sizes,
    query_hbm,
    key_hbm,
    value_hbm,
    grad_hbm,
    chain_ref,
    load_ref,
    length_ref,
    back_ref,
    rows_in,
    packed,
    landed,
    outgoing,
    load_own,
    load_all,
    spread,
    gathered,
    carry_low,
    onward_low,
    inside,
    inside_turned,
    root_wide,
    inner_wide,
    row_facts,
    queries,
    kept_queries,
    keys,
    kept_keys,
    values,
    kept_values,
    grads,
    dgrads,
    raw,
    extra_out,
    scores_turned,
    state_own,
    state_all,
    back_own,
    back_all,
    stage_one,
    stage_two,
    in_sem,
    load_sem,
    data_send,
    data_recv,
    state_send,
    state_recv,
    sum_send,
    sum_recv,
    out_send,
    out_recv,
):
    main, extra = sizes
    rows_all = 4 * (main + extra)
    main_slots = SOURCES * main
    slots = main_slots + SOURCES * extra
    tiles, parts = slots // TILE, slots // PART
    early, late = pl.ds(0, 3 * main + 4 * extra), pl.ds(3 * main + 4 * extra, main)
    place, x = lax.axis_index("ctx"), lax.axis_index("head")
    y, z, c = place // 16, lax.rem(place // 2, 8), lax.rem(place, 2)
    mine = y * 2 + c

    def wrapped(value, size):
        return jnp.where(value >= size, value - size, value)

    rows_y = [wrapped(y + n, 4) for n in range(4)]
    plane = []
    for j in range(8):
        cc = c if j % 2 == 0 else 1 - c
        plane.append((rows_y[j // 2] * 16 + cc, rows_y[j // 2] * 2 + cc))

    def at(j, zz):
        return plane[j][0] + 2 * zz, plane[j][1]

    def each_other(act):
        for j in range(1, 8):
            act(*at(j, z), z)

        def level(i, carry):
            zz = wrapped(z + i, 8)
            for j in range(8):
                act(*at(j, zz), zz)
            return carry

        lax.fori_loop(1, 8, level, 0)

    def remote(src, dst, send, recv, ctx, head):
        return pltpu.make_async_remote_copy(
            src_ref=src,
            dst_ref=dst,
            send_sem=send,
            recv_sem=recv,
            device_id=(ctx, head),
            device_id_type=MESH,
        )

    def settle(ref, sem):
        pltpu.make_async_copy(ref, ref, sem).wait()

    inputs = (query_hbm, key_hbm, value_hbm, grad_hbm)
    for a, source in enumerate(inputs):
        pltpu.make_async_copy(source, rows_in.at[pl.ds(a * TILE, TILE)], in_sem.at[a]).start()

    barrier = pltpu.get_barrier_semaphore()

    def greet(ctx, head, zz):
        pl.semaphore_signal(barrier, inc=1, device_id=(ctx, x), device_id_type=MESH)

    each_other(greet)
    for j in range(1, 4):
        pl.semaphore_signal(
            barrier, inc=1, device_id=(place, wrapped(x + j, 4)), device_id_type=MESH
        )

    group, rank = group_and_rank(chain_ref[...].astype(F32), 0)
    targets = []
    for a in range(4):
        main_row = (a * main if a < 3 else 3 * main + 4 * extra) + rank
        extra_row = 3 * main + a * extra + rank - main
        targets.append(group * rows_all + jnp.where(rank < main, main_row, extra_row))
    target = jnp.concatenate(targets, axis=1).astype(jnp.int32)
    load_own[...] = jnp.broadcast_to(load_ref[...], (8, TILE))
    for a, source in enumerate(inputs):
        pltpu.make_async_copy(source, rows_in.at[pl.ds(a * TILE, TILE)], in_sem.at[a]).wait()
    pl.semaphore_wait(barrier, 66)

    owner = place // 8
    for j in range(8):
        ctx, unused = at(j, owner)
        send = load_sem.at[1 if j == 0 else 0]
        if j == 0:

            @pl.when(owner == z)
            def _():
                pltpu.make_async_copy(
                    load_own, load_all.at[lax.rem(place, 8)], load_sem.at[2]
                ).start()

            @pl.when(owner != z)
            def _():
                remote(
                    load_own, load_all.at[lax.rem(place, 8)], send, load_sem.at[2], ctx, x
                ).start()
        else:
            remote(load_own, load_all.at[lax.rem(place, 8)], send, load_sem.at[2], ctx, x).start()

    row_number = iota((rows_all, 4 * TILE), 0)

    def send_rows(slot, ctx, rows, recv):
        remote(
            packed.at[slot, rows], landed.at[place, rows], data_send, data_recv.at[recv], ctx, x
        ).start()

    def keep_rows(slot, rows, recv):
        pltpu.make_async_copy(
            packed.at[slot, rows], landed.at[place, rows], data_recv.at[recv]
        ).start()

    def pack_group(i, carry):
        goal = wrapped(z + i + 1, 8)
        pick = ones_where(row_number + goal * rows_all == target).astype(LOW)
        block = nn(pick, rows_in[...]).astype(LOW)
        for head in range(HEADS_HERE):
            packed[goal * 8 + head] = block[:, head * TILE : (head + 1) * TILE]
        for j in range(8):
            ctx, head = at(j, goal)
            if j == 0:

                @pl.when(i < 7)
                def _():
                    send_rows(goal * 8 + head, ctx, early, 0)

            else:
                send_rows(goal * 8 + head, ctx, early, 0)
        return carry

    lax.fori_loop(0, 8, pack_group, 0)
    keep_rows(z * 8 + mine, early, 0)
    keep_rows(z * 8 + mine, late, 1)

    def send_late(ctx, head, zz):
        send_rows(zz * 8 + head, ctx, late, 1)

    each_other(send_late)

    down, across = iota((TILE, TILE), 0), iota((TILE, TILE), 1)
    lengths = jnp.broadcast_to(length_ref[...].astype(F32), (TILE, TILE))
    ends_down = jnp.sum(jnp.where(across <= down, lengths, 0.0), axis=1, keepdims=True)
    ends = jnp.transpose(jnp.broadcast_to(ends_down, (TILE, TILE)))
    base = (z * GROUP_TOKENS).astype(F32)
    top = base + float(GROUP_TOKENS)

    def goes_on(last_tokens, first):
        start = jnp.max(
            jnp.where(ends[0:1] <= last_tokens - 1.0, ends[0:1], 0.0), axis=1, keepdims=True
        )
        return ones_where(start < first)

    if extra:
        number, other = iota((PART, PART), 0), iota((PART, PART), 1)
        array, rest = number // 64, lax.rem(number, 64)
        goal = (rest // 4) * 16 + array * 4 + lax.rem(rest, 4)
        gathered[...] = ones_where(goal == other).astype(LOW)
        source, rest = number // 16, lax.rem(number, 16)
        origin = (rest // 4) * 64 + source * 4 + lax.rem(rest, 4)
        spread[...] = ones_where(origin == other).astype(LOW)

    settle(load_all, load_sem.at[2])
    below = ones_where(across < down).astype(LOW)
    slot_number = iota((TILE, slots), 1).astype(F32)
    fact_row, fact_lane = iota((8, TILE), 0), iota((8, TILE), 1)
    seen = jnp.zeros((1, TILE), F32)
    facts = jnp.zeros((8, slots), F32)
    for j in range(8):
        source = (load_all[j, 0:1] // TILE).astype(F32)
        source_wide = turned(source)
        same = ones_where(source_wide == across.astype(F32))
        earlier = nn(below, same.astype(LOW)) + seen
        place_in = jnp.sum(same * earlier, axis=1, keepdims=True)
        seen = seen + jnp.sum(same, axis=0, keepdims=True)
        source_column = source_wide[:, 0:1]
        slot = jnp.where(
            place_in < main,
            source_column * main + place_in,
            main_slots + source_column * extra + place_in - main,
        )
        pick = ones_where(slot == slot_number).astype(LOW)
        told = jnp.where(
            fact_row == 0, j, jnp.where(fact_row == 1, fact_lane, jnp.where(fact_row == 2, 1, 0))
        )
        facts = facts + nn(told.astype(F32).astype(LOW), pick)
    position = jnp.where(facts[2:3] > 0.5, base + facts[0:1] * TILE + facts[1:2], -1.0)
    row_facts[0:1] = position
    for t in range(tiles):
        tile = slice(t * TILE, (t + 1) * TILE)
        where = turned(position[:, tile])
        start = jnp.max(jnp.where(ends <= where, ends, 0.0), axis=1, keepdims=True)
        end = jnp.min(jnp.where(ends > where, ends, float(TOKENS)), axis=1, keepdims=True)
        start_all = jnp.broadcast_to(start, (TILE, TILE))
        end_all = jnp.broadcast_to(end, (TILE, TILE))
        carry_low[tile] = ones_where((start_all < base) & (where >= 0.0)).astype(LOW)
        onward_low[tile] = ones_where((end_all > top) & (where >= 0.0)).astype(LOW)
        reached = (position <= where[:, 0:1]) & (position >= start)
        inside[tile] = ones_where(reached).astype(LOW)
        row_facts[1:2, tile] = jnp.transpose(start_all)[0:1]
    for t in range(tiles):
        tile = slice(t * TILE, (t + 1) * TILE)
        where = turned(position[:, tile])[:, 0:1]
        reaching = (where <= position) & (where >= row_facts[1:2])
        inside_turned[tile] = ones_where(reaching).astype(LOW)

    def part(i):
        return pl.ds(pl.multiple_of(i * PART, PART), PART)

    settle(landed.at[:, early], data_recv.at[0])
    for a, ref in enumerate((queries, keys, values)):
        ref[0:main_slots] = landed[:, a * main : (a + 1) * main].reshape(main_slots, TILE)
    if extra:
        held = landed[:, 3 * main : 3 * main + 4 * extra].reshape(1024, TILE)
        side = jnp.concatenate([held[n * PART : (n + 1) * PART] for n in range(4)], axis=1)
        sorted_rows = nn(gathered[...], side).astype(LOW)
        for n in range(4):
            for a, ref in enumerate((queries, keys, values, grads)):
                ref[main_slots + n * 64 : main_slots + (n + 1) * 64] = sorted_rows[
                    a * 64 : (a + 1) * 64, n * TILE : (n + 1) * TILE
                ]

    kept_keys[...] = keys[...] * onward_low[...]
    state_own[...] = tn(kept_keys[...], values[...])
    for n in (1, 2):
        ctx, unused = at(0, wrapped(z + n, 8))
        remote(
            state_own, state_all.at[n - 1], state_send.at[0], state_recv.at[n - 1], ctx, x
        ).start()
    kept_queries[...] = queries[...] * carry_low[...]
    kept_values[...] = values[...] * onward_low[...]

    def forward_part(i, carry):
        rows = part(i)
        low = nt(queries[rows], keys[...]).astype(LOW) * inside[rows]
        raw[rows] = nn(low, values[...])
        return carry

    lax.fori_loop(0, parts, forward_part, 0)
    settle(state_all.at[0], state_recv.at[0])
    settle(state_all.at[1], state_recv.at[1])
    state = state_all[0] + goes_on(base, base - float(GROUP_TOKENS)) * state_all[1]
    state_low = state.astype(LOW)
    raw[...] = raw[...] + nn(kept_queries[...], state_low)

    def tile_sums(product):
        row = iota((16, TILE), 0)
        total = jnp.zeros((16, TILE), F32)
        ones = jnp.ones((16, TILE), LOW)
        for t in range(tiles):
            tile = product(slice(t * TILE, (t + 1) * TILE))
            high = tile.astype(LOW)
            rest = (tile - high.astype(F32)).astype(LOW)
            total = jnp.where(row == t, nt(ones, high) + nt(ones, rest), total)
        return total

    def head_sum_start(k, partial):
        stage_one[k, mine] = partial
        for j in range(1, 8):
            ctx, unused = at(j, z)
            remote(
                stage_one.at[k, mine],
                stage_one.at[k, mine],
                sum_send.at[2 * k],
                sum_recv.at[2 * k],
                ctx,
                x,
            ).start()

    def head_sum_next(k):
        settle(stage_one.at[k, pl.ds(0, 7)], sum_recv.at[2 * k])
        total = stage_one[k, 0]
        for j in range(1, 8):
            total = total + stage_one[k, j]
        stage_two[k, x] = total
        for j in range(1, 4):
            remote(
                stage_two.at[k, x],
                stage_two.at[k, x],
                sum_send.at[2 * k + 1],
                sum_recv.at[2 * k + 1],
                place,
                wrapped(x + j, 4),
            ).start()

    def head_sum_end(k):
        settle(stage_two.at[k, pl.ds(0, 3)], sum_recv.at[2 * k + 1])
        return (stage_two[k, 0] + stage_two[k, 1]) + (stage_two[k, 2] + stage_two[k, 3])

    head_sum_start(0, tile_sums(lambda tile: raw[tile] * raw[tile]))

    def turned_part(i, carry):
        rows = part(i)
        scores_turned[rows] = nt(keys[rows], queries[...]).astype(LOW) * inside_turned[rows]
        return carry

    lax.fori_loop(0, parts, turned_part, 0)
    head_sum_next(0)
    settle(landed.at[:, late], data_recv.at[1])
    grads[0:main_slots] = landed[:, late].reshape(main_slots, TILE)
    head_sum_start(1, tile_sums(lambda tile: raw[tile] * grads[tile].astype(F32)))
    total = head_sum_end(0)
    inverse = 1.0 / jnp.sqrt(total / FEATURES + epsilon)
    for t in range(tiles):
        root_wide[t * TILE : (t + 1) * TILE] = turned(inverse[t : t + 1])
    raw[...] = raw[...] * root_wide[...]

    def put(array, i, value):
        sources = PART // main
        if i < main_slots // PART:
            outgoing[i * sources : (i + 1) * sources, array * main : (array + 1) * main] = (
                value.reshape(sources, main, TILE)
            )
        else:
            extra_out[array * 256 : (array + 1) * 256] = value

    for i in range(parts):
        put(0, i, raw[i * PART : (i + 1) * PART].astype(LOW))
    head_sum_next(1)

    def send_back(rows):
        def one(ctx, head, zz):
            remote(
                outgoing.at[ctx, rows], back_ref.at[z, mine, rows], out_send, out_recv, ctx, x
            ).start()

        each_other(one)
        pltpu.make_async_copy(
            outgoing.at[place, rows], back_ref.at[z, mine, rows], out_recv
        ).start()

    send_back(pl.ds(0, main))
    inner = head_sum_end(1) * inverse / FEATURES
    for t in range(tiles):
        inner_wide[t * TILE : (t + 1) * TILE] = turned(inner[t : t + 1])
    dgrads[...] = (
        (grads[...].astype(F32) - raw[...] * inner_wide[...]) * root_wide[...]
    ).astype(LOW)

    back_own[...] = tn(kept_queries[...], dgrads[...])
    for n in (1, 2):
        ctx, unused = at(0, wrapped(z + 8 - n, 8))
        remote(
            back_own, back_all.at[n - 1], state_send.at[1], state_recv.at[n + 1], ctx, x
        ).start()

    for i in range(parts):
        rows = slice(i * PART, (i + 1) * PART)
        mixed = nt(dgrads[rows], values[...]).astype(LOW) * inside[rows]
        kept = dgrads[rows] * carry_low[rows]
        put(1, i, (nn(mixed, keys[...]) + nt(kept, state_low)).astype(LOW))
    send_back(pl.ds(main, main))

    settle(back_all.at[0], state_recv.at[2])
    settle(back_all.at[1], state_recv.at[3])
    back = back_all[0] + goes_on(top + float(GROUP_TOKENS), top) * back_all[1]
    back_low = back.astype(LOW)
    for i in range(parts):
        rows = slice(i * PART, (i + 1) * PART)
        mixed = nt(values[rows], dgrads[...]).astype(LOW) * inside_turned[rows]
        put(2, i, (nn(mixed, queries[...]) + nt(kept_values[rows], back_low)).astype(LOW))
        value_part = nn(scores_turned[rows], dgrads[...]) + nn(kept_keys[rows], back_low)
        put(3, i, value_part.astype(LOW))
    if extra:
        held = extra_out[...]
        blocks = []
        for n in range(4):
            pieces = [held[a * 256 + n * 64 : a * 256 + (n + 1) * 64] for a in range(4)]
            blocks.append(jnp.concatenate(pieces, axis=0))
        extra_rows = nn(spread[...], jnp.concatenate(blocks, axis=1)).astype(LOW)
        for n in range(4):
            outgoing[n * 16 : (n + 1) * 16, 4 * main : rows_all] = extra_rows[
                :, n * TILE : (n + 1) * TILE
            ].reshape(16, 4 * extra, TILE)
    send_back(pl.ds(2 * main, 2 * main + 4 * extra))

    settle(load_all.at[pl.ds(0, 7)], load_sem.at[0])

    @pl.when(owner != z)
    def _():
        settle(load_own, load_sem.at[1])

    settle(packed.at[pl.ds(0, 63)], data_send)
    settle(state_all, state_send.at[0])
    settle(back_all, state_send.at[1])
    for k in range(2):
        settle(stage_one.at[k, pl.ds(0, 7)], sum_send.at[2 * k])
        settle(stage_two.at[k, pl.ds(0, 3)], sum_send.at[2 * k + 1])
    settle(outgoing.at[pl.ds(0, 63)], out_send)
    settle(outgoing, out_recv)


def unpack_kernel(sizes, chain_ref, back_ref, attended_ref, query_ref, key_ref, value_ref):
    main, extra = sizes
    rows_all = 4 * (main + extra)
    group, rank = group_and_rank(chain_ref[...].astype(F32), 1)
    number = iota((TILE, GROUPS * rows_all), 1).astype(F32)
    picks = []
    for a in range(4):
        row = jnp.where(rank < main, a * main + rank, 4 * main + a * extra + rank - main)
        picks.append(ones_where(group * rows_all + row == number).astype(LOW))
    pick = jnp.concatenate(picks, axis=0)
    for head in range(HEADS_HERE):
        found = nn(pick, back_ref[:, head].reshape(GROUPS * rows_all, TILE)).astype(LOW)
        lanes = slice(head * TILE, (head + 1) * TILE)
        for a, ref in enumerate((attended_ref, query_ref, key_ref, value_ref)):
            ref[:, lanes] = found[a * TILE : (a + 1) * TILE]


def layer(sizes, query_in, key_in, value_in, out_grad, chain_order, load_order, doc_lengths):
    main, extra = sizes
    rows_all, slots = 4 * (main + extra), SOURCES * (main + extra)
    chain_row = chain_order.reshape(1, TILE)
    whole = pl.BlockSpec(memory_space=pltpu.VMEM)
    anywhere = pl.BlockSpec(memory_space=pl.ANY)
    wide = pltpu.VMEM((slots, TILE), F32)
    low = pltpu.VMEM((slots, TILE), LOW)
    square = pltpu.VMEM((slots, slots), LOW)
    blocks = pltpu.VMEM((SOURCES, rows_all, TILE), LOW)
    dma = pltpu.SemaphoreType.DMA
    returned = pl.pallas_call(
        functools.partial(fused_kernel, sizes),
        out_shape=jax.ShapeDtypeStruct((GROUPS, HEADS_HERE, rows_all, TILE), LOW),
        in_specs=[anywhere] * 4 + [whole] * 3,
        out_specs=anywhere,
        scratch_shapes=[
            pltpu.VMEM((4 * TILE, HEADS_HERE * TILE), LOW),
            blocks,
            blocks,
            blocks,
            pltpu.VMEM((8, TILE), jnp.int32),
            pltpu.VMEM((8, 8, TILE), jnp.int32),
            pltpu.VMEM((PART, PART), LOW),
            pltpu.VMEM((PART, PART), LOW),
            low,
            low,
            square,
            square,
            wide,
            wide,
            pltpu.VMEM((8, slots), F32),
            low,
            low,
            low,
            low,
            low,
            low,
            low,
            low,
            wide,
            pltpu.VMEM((1024, TILE), LOW),
            square,
            pltpu.VMEM((TILE, TILE), F32),
            pltpu.VMEM((2, TILE, TILE), F32),
            pltpu.VMEM((TILE, TILE), F32),
            pltpu.VMEM((2, TILE, TILE), F32),
            pltpu.VMEM((2, 8, 16, TILE), F32),
            pltpu.VMEM((2, 4, 16, TILE), F32),
            dma((4,)),
            dma((3,)),
            dma,
            dma((2,)),
            dma((2,)),
            dma((4,)),
            dma((4,)),
            dma((4,)),
            dma,
            dma,
        ],
        compiler_params=pltpu.CompilerParams(
            collective_id=1 if extra else 2, has_side_effects=True, vmem_limit_bytes=62 << 20
        ),
        name="fused",
    )(
        query_in,
        key_in,
        value_in,
        out_grad,
        chain_row,
        load_order.reshape(1, TILE),
        doc_lengths.reshape(1, TILE),
    )
    out = jax.ShapeDtypeStruct((TILE, HEADS_HERE * TILE), LOW)
    return pl.pallas_call(
        functools.partial(unpack_kernel, sizes),
        out_shape=(out,) * 4,
        in_specs=[whole] * 2,
        out_specs=(whole,) * 4,
        compiler_params=pltpu.CompilerParams(vmem_limit_bytes=62 << 20),
        name="unpack",
    )(chain_row, returned)


def body(query_in, key_in, value_in, out_grad, chain_order, load_order, doc_lengths):
    ahead = jnp.mod(chain_order // TILE - lax.axis_index("ctx"), SOURCES)
    windows = jnp.mod(ahead[None, :] - jnp.arange(SOURCES)[:, None], SOURCES) < GROUPS
    most = jnp.max(jnp.sum(windows.astype(jnp.int32), axis=1))
    return lax.cond(
        most <= sum(SMALL),
        functools.partial(layer, SMALL),
        functools.partial(layer, LARGE),
        query_in,
        key_in,
        value_in,
        out_grad,
        chain_order,
        load_order,
        doc_lengths,
    )


def solution(mesh):
    return jax.shard_map(
        body,
        mesh=mesh,
        in_specs=(
            P("ctx", "head"),
            P("ctx", "head"),
            P("ctx", "head"),
            P("ctx", "head"),
            P("ctx"),
            P("ctx"),
            P(),
        ),
        out_specs=(P("ctx", "head"), P("ctx", "head"), P("ctx", "head"), P("ctx", "head")),
        check_vma=False,
    )
```

```python
import functools
import jax
import jax.numpy as jnp
from jax import lax
from jax.experimental import pallas as pl
from jax.experimental.pallas import tpu as pltpu
from jax.sharding import PartitionSpec as P

HEAD_DIM = 128
FEATURES = 4096

epsilon = 1e-06

SOURCES = 64
GROUPS = 8
GROUP_TOKENS = 1024
TILE = 128
PART = 256
TOKENS = 8192
HEADS_HERE = 8
SMALL = (16, 4)
LARGE = (32, 0)
MESH = pl.DeviceIdType.MESH
F32 = jnp.float32
LOW = jnp.bfloat16


def nn(left, right, precision=None):
    return lax.dot_general(
        left, right, (((1,), (0,)), ((), ())), precision=precision, preferred_element_type=F32
    )


def nt(left, right, precision=None):
    return lax.dot_general(
        left, right, (((1,), (1,)), ((), ())), precision=precision, preferred_element_type=F32
    )


def tn(left, right):
    return lax.dot_general(left, right, (((0,), (0,)), ((), ())), preferred_element_type=F32)


def iota(shape, dim):
    return lax.broadcasted_iota(jnp.int32, shape, dim)


def turned(row):
    return jnp.transpose(jnp.broadcast_to(row, (TILE, TILE)))


def ones_where(mask):
    return jnp.where(mask, 1.0, 0.0)


def group_and_rank(chain_row, axis):
    across = jnp.broadcast_to(chain_row, (TILE, TILE))
    down = jnp.transpose(across)
    group_across = jnp.floor(across * (1.0 / GROUP_TOKENS))
    group_down = jnp.floor(down * (1.0 / GROUP_TOKENS))
    same = group_across == group_down
    if axis == 0:
        rank = jnp.sum(ones_where(same & (down < across)), axis=0, keepdims=True)
        return group_across[0:1], rank
    rank = jnp.sum(ones_where(same & (across < down)), axis=1, keepdims=True)
    return group_down[:, 0:1], rank


def fused_kernel(
    sizes,
    query_hbm,
    key_hbm,
    value_hbm,
    grad_hbm,
    chain_ref,
    load_ref,
    length_ref,
    back_ref,
    roots_ref,
    rows_in,
    packed,
    landed,
    outgoing,
    load_own,
    load_all,
    spread,
    gathered,
    carry_low,
    onward_low,
    inside,
    inside_turned,
    root_wide,
    inner_wide,
    row_facts,
    queries,
    kept_queries,
    keys,
    kept_keys,
    values,
    kept_values,
    grads,
    dgrads,
    raw,
    extra_out,
    scores_turned,
    state_own,
    state_all,
    back_own,
    back_all,
    stage_one,
    stage_two,
    root_tile,
    root_sem,
    in_sem,
    load_sem,
    data_send,
    data_recv,
    state_send,
    state_recv,
    sum_send,
    sum_recv,
    out_send,
    out_recv,
):
    main, extra = sizes
    rows_all = 4 * (main + extra)
    main_slots = SOURCES * main
    slots = main_slots + SOURCES * extra
    tiles, parts = slots // TILE, slots // PART
    early, late = pl.ds(0, 3 * main + 4 * extra), pl.ds(3 * main + 4 * extra, main)
    place, x = lax.axis_index("ctx"), lax.axis_index("head")
    y, z, c = place // 16, lax.rem(place // 2, 8), lax.rem(place, 2)
    mine = y * 2 + c

    def wrapped(value, size):
        return jnp.where(value >= size, value - size, value)

    rows_y = [wrapped(y + n, 4) for n in range(4)]
    plane = []
    for j in range(8):
        cc = c if j % 2 == 0 else 1 - c
        plane.append((rows_y[j // 2] * 16 + cc, rows_y[j // 2] * 2 + cc))

    def at(j, zz):
        return plane[j][0] + 2 * zz, plane[j][1]

    def height(i):
        half = (i + 1) // 2
        return wrapped(z + jnp.where(lax.rem(i, 2) == 1, 4 - half, 4 + half), 8)

    def each_other(act):
        def level(i, carry):
            zz = height(i)
            for j in range(8):
                act(*at(j, zz), zz)
            return carry

        lax.fori_loop(0, 7, level, 0)
        for j in range(1, 8):
            act(*at(j, z), z)

    def remote(src, dst, send, recv, ctx, head):
        return pltpu.make_async_remote_copy(
            src_ref=src,
            dst_ref=dst,
            send_sem=send,
            recv_sem=recv,
            device_id=(ctx, head),
            device_id_type=MESH,
        )

    def settle(ref, sem):
        pltpu.make_async_copy(ref, ref, sem).wait()

    inputs = (query_hbm, key_hbm, value_hbm, grad_hbm)
    for a, source in enumerate(inputs):
        pltpu.make_async_copy(source, rows_in.at[pl.ds(a * TILE, TILE)], in_sem.at[a]).start()

    barrier = pltpu.get_barrier_semaphore()

    def greet(ctx, head, zz):
        pl.semaphore_signal(barrier, inc=1, device_id=(ctx, x), device_id_type=MESH)

    each_other(greet)
    for j in range(1, 4):
        pl.semaphore_signal(
            barrier, inc=1, device_id=(place, wrapped(x + j, 4)), device_id_type=MESH
        )

    group, rank = group_and_rank(chain_ref[...].astype(F32), 0)
    targets = []
    for a in range(4):
        main_row = (a * main if a < 3 else 3 * main + 4 * extra) + rank
        extra_row = 3 * main + a * extra + rank - main
        targets.append(group * rows_all + jnp.where(rank < main, main_row, extra_row))
    target = jnp.concatenate(targets, axis=1).astype(jnp.int32)
    load_own[...] = jnp.broadcast_to(load_ref[...], (8, TILE))
    for a, source in enumerate(inputs):
        pltpu.make_async_copy(source, rows_in.at[pl.ds(a * TILE, TILE)], in_sem.at[a]).wait()
    pl.semaphore_wait(barrier, 66)

    owner = place // 8
    for j in range(8):
        ctx, unused = at(j, owner)
        send = load_sem.at[1 if j == 0 else 0]
        if j == 0:

            @pl.when(owner == z)
            def _():
                pltpu.make_async_copy(
                    load_own, load_all.at[lax.rem(place, 8)], load_sem.at[2]
                ).start()

            @pl.when(owner != z)
            def _():
                remote(
                    load_own, load_all.at[lax.rem(place, 8)], send, load_sem.at[2], ctx, x
                ).start()
        else:
            remote(load_own, load_all.at[lax.rem(place, 8)], send, load_sem.at[2], ctx, x).start()

    row_number = iota((rows_all, 4 * TILE), 0)

    def send_rows(slot, ctx, rows, recv):
        remote(
            packed.at[slot, rows], landed.at[place, rows], data_send, data_recv.at[recv], ctx, x
        ).start()

    def keep_rows(slot, rows, recv):
        pltpu.make_async_copy(
            packed.at[slot, rows], landed.at[place, rows], data_recv.at[recv]
        ).start()

    def pack_group(i, carry):
        goal = height(i)
        pick = ones_where(row_number + goal * rows_all == target).astype(LOW)
        block = nn(pick, rows_in[...]).astype(LOW)
        for head in range(HEADS_HERE):
            packed[goal * 8 + head] = block[:, head * TILE : (head + 1) * TILE]
        for j in range(8):
            ctx, head = at(j, goal)
            if j == 0:

                @pl.when(i < 7)
                def _():
                    send_rows(goal * 8 + head, ctx, early, 0)

            else:
                send_rows(goal * 8 + head, ctx, early, 0)
        return carry

    lax.fori_loop(0, 8, pack_group, 0)
    keep_rows(z * 8 + mine, early, 0)
    keep_rows(z * 8 + mine, late, 1)

    def send_late(ctx, head, zz):
        send_rows(zz * 8 + head, ctx, late, 1)

    each_other(send_late)

    down, across = iota((TILE, TILE), 0), iota((TILE, TILE), 1)
    lengths = jnp.broadcast_to(length_ref[...].astype(F32), (TILE, TILE))
    ends_down = jnp.sum(jnp.where(across <= down, lengths, 0.0), axis=1, keepdims=True)
    ends = jnp.transpose(jnp.broadcast_to(ends_down, (TILE, TILE)))
    base = (z * GROUP_TOKENS).astype(F32)
    top = base + float(GROUP_TOKENS)

    def goes_on(last_tokens, first):
        start = jnp.max(
            jnp.where(ends[0:1] <= last_tokens - 1.0, ends[0:1], 0.0), axis=1, keepdims=True
        )
        return ones_where(start < first)

    if extra:
        number, other = iota((PART, PART), 0), iota((PART, PART), 1)
        array, rest = number // 64, lax.rem(number, 64)
        goal = (rest // 4) * 16 + array * 4 + lax.rem(rest, 4)
        gathered[...] = ones_where(goal == other).astype(LOW)
        source, rest = number // 16, lax.rem(number, 16)
        origin = (rest // 4) * 64 + source * 4 + lax.rem(rest, 4)
        spread[...] = ones_where(origin == other).astype(LOW)

    settle(load_all, load_sem.at[2])
    below = ones_where(across < down).astype(LOW)
    slot_number = iota((TILE, slots), 1).astype(F32)
    fact_row, fact_lane = iota((8, TILE), 0), iota((8, TILE), 1)
    seen = jnp.zeros((1, TILE), F32)
    facts = jnp.zeros((8, slots), F32)
    for j in range(8):
        source = (load_all[j, 0:1] // TILE).astype(F32)
        source_wide = turned(source)
        same = ones_where(source_wide == across.astype(F32))
        earlier = nn(below, same.astype(LOW)) + seen
        place_in = jnp.sum(same * earlier, axis=1, keepdims=True)
        seen = seen + jnp.sum(same, axis=0, keepdims=True)
        source_column = source_wide[:, 0:1]
        slot = jnp.where(
            place_in < main,
            source_column * main + place_in,
            main_slots + source_column * extra + place_in - main,
        )
        pick = ones_where(slot == slot_number).astype(LOW)
        told = jnp.where(
            fact_row == 0, j, jnp.where(fact_row == 1, fact_lane, jnp.where(fact_row == 2, 1, 0))
        )
        facts = facts + nn(told.astype(F32).astype(LOW), pick)
    position = jnp.where(facts[2:3] > 0.5, base + facts[0:1] * TILE + facts[1:2], -1.0)
    row_facts[0:1] = position
    for t in range(tiles):
        tile = slice(t * TILE, (t + 1) * TILE)
        where = turned(position[:, tile])
        start = jnp.max(jnp.where(ends <= where, ends, 0.0), axis=1, keepdims=True)
        end = jnp.min(jnp.where(ends > where, ends, float(TOKENS)), axis=1, keepdims=True)
        start_all = jnp.broadcast_to(start, (TILE, TILE))
        end_all = jnp.broadcast_to(end, (TILE, TILE))
        carry_low[tile] = ones_where((start_all < base) & (where >= 0.0)).astype(LOW)
        onward_low[tile] = ones_where((end_all > top) & (where >= 0.0)).astype(LOW)
        reached = (position <= where[:, 0:1]) & (position >= start)
        inside[tile] = ones_where(reached).astype(LOW)
        row_facts[1:2, tile] = jnp.transpose(start_all)[0:1]
    for t in range(tiles):
        tile = slice(t * TILE, (t + 1) * TILE)
        where = turned(position[:, tile])[:, 0:1]
        reaching = (where <= position) & (where >= row_facts[1:2])
        inside_turned[tile] = ones_where(reaching).astype(LOW)

    def part(i):
        return pl.ds(pl.multiple_of(i * PART, PART), PART)

    settle(landed.at[:, early], data_recv.at[0])
    for a, ref in enumerate((queries, keys, values)):
        ref[0:main_slots] = landed[:, a * main : (a + 1) * main].reshape(main_slots, TILE)
    if extra:
        held = landed[:, 3 * main : 3 * main + 4 * extra].reshape(1024, TILE)
        side = jnp.concatenate([held[n * PART : (n + 1) * PART] for n in range(4)], axis=1)
        sorted_rows = nn(gathered[...], side).astype(LOW)
        for n in range(4):
            for a, ref in enumerate((queries, keys, values, grads)):
                ref[main_slots + n * 64 : main_slots + (n + 1) * 64] = sorted_rows[
                    a * 64 : (a + 1) * 64, n * TILE : (n + 1) * TILE
                ]

    kept_keys[...] = keys[...] * onward_low[...]
    state_own[...] = tn(kept_keys[...], values[...]).astype(LOW)
    for n in (1, 2):
        ctx, unused = at(0, wrapped(z + n, 8))
        remote(
            state_own, state_all.at[n - 1], state_send.at[0], state_recv.at[n - 1], ctx, x
        ).start()
    kept_queries[...] = queries[...] * carry_low[...]
    kept_values[...] = values[...] * onward_low[...]

    def forward_part(i, carry):
        rows = part(i)
        low = nt(queries[rows], keys[...]).astype(LOW) * inside[rows]
        raw[rows] = nn(low, values[...])
        return carry

    lax.fori_loop(0, parts, forward_part, 0)
    settle(state_all.at[0], state_recv.at[0])
    settle(state_all.at[1], state_recv.at[1])
    before = goes_on(base, base - float(GROUP_TOKENS))
    state = state_all[0].astype(F32) + before * state_all[1].astype(F32)
    state_low = state.astype(LOW)

    def put(array, i, value):
        sources = PART // main
        if i < main_slots // PART:
            outgoing[i * sources : (i + 1) * sources, array * main : (array + 1) * main] = (
                value.reshape(sources, main, TILE)
            )
        else:
            extra_out[array * 256 : (array + 1) * 256] = value

    def send_back(rows):
        def one(ctx, head, zz):
            remote(
                outgoing.at[ctx, rows], back_ref.at[z, mine, rows], out_send, out_recv, ctx, x
            ).start()

        each_other(one)
        pltpu.make_async_copy(
            outgoing.at[place, rows], back_ref.at[z, mine, rows], out_recv
        ).start()

    for i in range(parts):
        rows = slice(i * PART, (i + 1) * PART)
        whole = raw[rows] + nn(kept_queries[rows], state_low)
        raw[rows] = whole
        put(0, i, whole.astype(LOW))
    send_back(pl.ds(0, main))

    def tile_sums(product):
        row = iota((16, TILE), 0)
        total = jnp.zeros((16, TILE), F32)
        ones = jnp.ones((16, TILE), LOW)
        for t in range(tiles):
            tile = product(slice(t * TILE, (t + 1) * TILE))
            high = tile.astype(LOW)
            rest = (tile - high.astype(F32)).astype(LOW)
            total = jnp.where(row == t, nt(ones, high) + nt(ones, rest), total)
        return total

    settle(landed.at[:, late], data_recv.at[1])
    grads[0:main_slots] = landed[:, late].reshape(main_slots, TILE)
    stage_one[mine, 0] = tile_sums(lambda tile: raw[tile] * raw[tile])
    stage_one[mine, 1] = tile_sums(lambda tile: raw[tile] * grads[tile].astype(F32))
    for j in range(1, 8):
        ctx, unused = at(j, z)
        own = stage_one.at[mine]
        remote(own, own, sum_send.at[0], sum_recv.at[0], ctx, x).start()

    def turned_part(i, carry):
        rows = part(i)
        scores_turned[rows] = nt(keys[rows], queries[...]).astype(LOW) * inside_turned[rows]
        return carry

    lax.fori_loop(0, parts, turned_part, 0)
    settle(stage_one.at[pl.ds(0, 7)], sum_recv.at[0])
    partial = stage_one[0]
    for j in range(1, 8):
        partial = partial + stage_one[j]
    stage_two[x] = partial
    for j in range(1, 4):
        own = stage_two.at[x]
        remote(own, own, sum_send.at[1], sum_recv.at[1], place, wrapped(x + j, 4)).start()
    settle(stage_two.at[pl.ds(0, 3)], sum_recv.at[1])
    total = (stage_two[0] + stage_two[1]) + (stage_two[2] + stage_two[3])
    inverse = 1.0 / jnp.sqrt(total[0] / FEATURES + epsilon)
    inner = total[1] * inverse / FEATURES
    root_tile[...] = inverse
    scale = inverse * inner
    for t in range(tiles):
        root_wide[t * TILE : (t + 1) * TILE] = turned(inverse[t : t + 1])
        inner_wide[t * TILE : (t + 1) * TILE] = turned(scale[t : t + 1])
    dgrads[...] = (
        (grads[...].astype(F32) - raw[...] * inner_wide[...]) * root_wide[...]
    ).astype(LOW)

    back_own[...] = tn(kept_queries[...], dgrads[...]).astype(LOW)
    for n in (1, 2):
        ctx, unused = at(0, wrapped(z + 8 - n, 8))
        remote(
            back_own, back_all.at[n - 1], state_send.at[1], state_recv.at[n + 1], ctx, x
        ).start()

    for j in range(8):
        ctx = wrapped(place // 8 + j, 8) * 8 + mine
        if j == 0:

            @pl.when(ctx == place)
            def _():
                pltpu.make_async_copy(root_tile, roots_ref.at[z], root_sem.at[2]).start()

            @pl.when(ctx != place)
            def _():
                remote(
                    root_tile, roots_ref.at[z], root_sem.at[1], root_sem.at[2], ctx, x
                ).start()
        else:
            remote(root_tile, roots_ref.at[z], root_sem.at[0], root_sem.at[2], ctx, x).start()

    for i in range(parts):
        rows = slice(i * PART, (i + 1) * PART)
        mixed = nt(dgrads[rows], values[...]).astype(LOW) * inside[rows]
        kept = dgrads[rows] * carry_low[rows]
        put(1, i, (nn(mixed, keys[...]) + nt(kept, state_low)).astype(LOW))
    send_back(pl.ds(main, main))

    settle(back_all.at[0], state_recv.at[2])
    settle(back_all.at[1], state_recv.at[3])
    after = goes_on(top + float(GROUP_TOKENS), top)
    back = back_all[0].astype(F32) + after * back_all[1].astype(F32)
    back_low = back.astype(LOW)
    for i in range(parts):
        rows = slice(i * PART, (i + 1) * PART)
        mixed = nt(values[rows], dgrads[...]).astype(LOW) * inside_turned[rows]
        put(2, i, (nn(mixed, queries[...]) + nt(kept_values[rows], back_low)).astype(LOW))
        value_part = nn(scores_turned[rows], dgrads[...]) + nn(kept_keys[rows], back_low)
        put(3, i, value_part.astype(LOW))
    if extra:
        held = extra_out[...]
        blocks = []
        for n in range(4):
            pieces = [held[a * 256 + n * 64 : a * 256 + (n + 1) * 64] for a in range(4)]
            blocks.append(jnp.concatenate(pieces, axis=0))
        extra_rows = nn(spread[...], jnp.concatenate(blocks, axis=1)).astype(LOW)
        for n in range(4):
            outgoing[n * 16 : (n + 1) * 16, 4 * main : rows_all] = extra_rows[
                :, n * TILE : (n + 1) * TILE
            ].reshape(16, 4 * extra, TILE)
    send_back(pl.ds(2 * main, 2 * main + 4 * extra))

    settle(load_all.at[pl.ds(0, 7)], load_sem.at[0])

    @pl.when(owner != z)
    def _():
        settle(load_own, load_sem.at[1])

    settle(packed.at[pl.ds(0, 63)], data_send)
    settle(state_all, state_send.at[0])
    settle(back_all, state_send.at[1])
    settle(stage_one.at[pl.ds(0, 7)], sum_send.at[0])
    settle(stage_two.at[pl.ds(0, 3)], sum_send.at[1])
    settle(roots_ref.at[pl.ds(0, 7)], root_sem.at[0])

    @pl.when(wrapped(place // 8, 8) * 8 + mine != place)
    def _():
        settle(root_tile, root_sem.at[1])

    settle(roots_ref, root_sem.at[2])
    settle(outgoing.at[pl.ds(0, 63)], out_send)
    settle(outgoing, out_recv)


def unpack_kernel(
    sizes, chain_ref, back_ref, roots_ref, attended_ref, query_ref, key_ref, value_ref, pick, factor
):
    main, extra = sizes
    rows_all = 4 * (main + extra)

    @pl.when(pl.program_id(0) == 0)
    def _():
        place = lax.axis_index("ctx")
        group, rank = group_and_rank(chain_ref[...].astype(F32), 1)
        number = iota((TILE, GROUPS * rows_all), 1).astype(F32)
        for a in range(4):
            row = jnp.where(rank < main, a * main + rank, 4 * main + a * extra + rank - main)
            pick[a * TILE : (a + 1) * TILE] = ones_where(
                group * rows_all + row == number
            ).astype(LOW)
        lane = iota((TILE, TILE), 1).astype(F32)
        kinds = [(place * main, rank, rank < main)]
        if extra:
            kinds.append((SOURCES * main + place * extra, rank - main, rank >= main))
        found = jnp.zeros((TILE, TILE), F32)
        for first, at_slot, chosen in kinds:
            wanted = jnp.where(chosen, lax.rem(first, TILE).astype(F32) + at_slot, -1.0)
            for g in range(GROUPS):
                row = roots_ref[g, pl.ds(first // TILE, 1)]
                found = found + jnp.where((group == g) & (wanted == lane), row, 0.0)
        factor[...] = jnp.broadcast_to(jnp.sum(found, axis=1, keepdims=True), (TILE, TILE))

    for head in range(2):
        found = nn(pick[...], back_ref[:, head].reshape(GROUPS * rows_all, TILE))
        lanes = slice(head * TILE, (head + 1) * TILE)
        attended_ref[:, lanes] = (found[0:TILE] * factor[...]).astype(LOW)
        for a, ref in enumerate((query_ref, key_ref, value_ref)):
            ref[:, lanes] = found[(a + 1) * TILE : (a + 2) * TILE].astype(LOW)


def layer(sizes, query_in, key_in, value_in, out_grad, chain_order, load_order, doc_lengths):
    main, extra = sizes
    rows_all, slots = 4 * (main + extra), SOURCES * (main + extra)
    chain_row = chain_order.reshape(1, TILE)
    whole = pl.BlockSpec(memory_space=pltpu.VMEM)
    anywhere = pl.BlockSpec(memory_space=pl.ANY)
    wide = pltpu.VMEM((slots, TILE), F32)
    low = pltpu.VMEM((slots, TILE), LOW)
    square = pltpu.VMEM((slots, slots), LOW)
    blocks = pltpu.VMEM((SOURCES, rows_all, TILE), LOW)
    dma = pltpu.SemaphoreType.DMA
    returned, roots = pl.pallas_call(
        functools.partial(fused_kernel, sizes),
        out_shape=(
            jax.ShapeDtypeStruct((GROUPS, HEADS_HERE, rows_all, TILE), LOW),
            jax.ShapeDtypeStruct((GROUPS, 16, TILE), F32),
        ),
        in_specs=[anywhere] * 4 + [whole] * 3,
        out_specs=(anywhere, anywhere),
        scratch_shapes=[
            pltpu.VMEM((4 * TILE, HEADS_HERE * TILE), LOW),
            blocks,
            blocks,
            blocks,
            pltpu.VMEM((8, TILE), jnp.int32),
            pltpu.VMEM((8, 8, TILE), jnp.int32),
            pltpu.VMEM((PART, PART), LOW),
            pltpu.VMEM((PART, PART), LOW),
            low,
            low,
            square,
            square,
            wide,
            wide,
            pltpu.VMEM((8, slots), F32),
            low,
            low,
            low,
            low,
            low,
            low,
            low,
            low,
            wide,
            pltpu.VMEM((1024, TILE), LOW),
            square,
            pltpu.VMEM((TILE, TILE), LOW),
            pltpu.VMEM((2, TILE, TILE), LOW),
            pltpu.VMEM((TILE, TILE), LOW),
            pltpu.VMEM((2, TILE, TILE), LOW),
            pltpu.VMEM((8, 2, 16, TILE), F32),
            pltpu.VMEM((4, 2, 16, TILE), F32),
            pltpu.VMEM((16, TILE), F32),
            dma((3,)),
            dma((4,)),
            dma((3,)),
            dma,
            dma((2,)),
            dma((2,)),
            dma((4,)),
            dma((2,)),
            dma((2,)),
            dma,
            dma,
        ],
        compiler_params=pltpu.CompilerParams(
            collective_id=1 if extra else 2, has_side_effects=True, vmem_limit_bytes=62 << 20
        ),
        name="fused",
    )(
        query_in,
        key_in,
        value_in,
        out_grad,
        chain_row,
        load_order.reshape(1, TILE),
        doc_lengths.reshape(1, TILE),
    )
    out = jax.ShapeDtypeStruct((TILE, HEADS_HERE * TILE), LOW)
    out_block = pl.BlockSpec((TILE, 2 * TILE), lambda i: (0, i))
    return pl.pallas_call(
        functools.partial(unpack_kernel, sizes),
        grid=(HEADS_HERE // 2,),
        out_shape=(out,) * 4,
        in_specs=[
            pl.BlockSpec((1, TILE), lambda i: (0, 0)),
            pl.BlockSpec((GROUPS, 2, rows_all, TILE), lambda i: (0, i, 0, 0)),
            pl.BlockSpec((GROUPS, 16, TILE), lambda i: (0, 0, 0)),
        ],
        out_specs=(out_block,) * 4,
        scratch_shapes=[
            pltpu.VMEM((4 * TILE, GROUPS * rows_all), LOW),
            pltpu.VMEM((TILE, TILE), F32),
        ],
        compiler_params=pltpu.CompilerParams(vmem_limit_bytes=62 << 20),
        name="unpack",
    )(chain_row, returned, roots)


def body(query_in, key_in, value_in, out_grad, chain_order, load_order, doc_lengths):
    ahead = jnp.mod(chain_order // TILE - lax.axis_index("ctx"), SOURCES)
    windows = jnp.mod(ahead[None, :] - jnp.arange(SOURCES)[:, None], SOURCES) < GROUPS
    most = jnp.max(jnp.sum(windows.astype(jnp.int32), axis=1))
    return lax.cond(
        most <= sum(SMALL),
        functools.partial(layer, SMALL),
        functools.partial(layer, LARGE),
        query_in,
        key_in,
        value_in,
        out_grad,
        chain_order,
        load_order,
        doc_lengths,
    )


def solution(mesh):
    return jax.shard_map(
        body,
        mesh=mesh,
        in_specs=(
            P("ctx", "head"),
            P("ctx", "head"),
            P("ctx", "head"),
            P("ctx", "head"),
            P("ctx"),
            P("ctx"),
            P(),
        ),
        out_specs=(P("ctx", "head"), P("ctx", "head"), P("ctx", "head"), P("ctx", "head")),
        check_vma=False,
    )
```

```python
import functools
import jax
import jax.numpy as jnp
from jax import lax
from jax.experimental import pallas as pl
from jax.experimental.pallas import tpu as pltpu
from jax.sharding import PartitionSpec as P

HEAD_DIM = 128
FEATURES = 4096

epsilon = 1e-06

SOURCES = 64
GROUPS = 8
GROUP_TOKENS = 1024
TILE = 128
PART = 256
TOKENS = 8192
HEADS_HERE = 8
SMALL = (16, 4)
LARGE = (32, 0)
MESH = pl.DeviceIdType.MESH
F32 = jnp.float32
LOW = jnp.bfloat16


def nn(left, right, precision=None):
    return lax.dot_general(
        left, right, (((1,), (0,)), ((), ())), precision=precision, preferred_element_type=F32
    )


def nt(left, right, precision=None):
    return lax.dot_general(
        left, right, (((1,), (1,)), ((), ())), precision=precision, preferred_element_type=F32
    )


def tn(left, right):
    return lax.dot_general(left, right, (((0,), (0,)), ((), ())), preferred_element_type=F32)


def iota(shape, dim):
    return lax.broadcasted_iota(jnp.int32, shape, dim)


def turned(row):
    return jnp.transpose(jnp.broadcast_to(row, (TILE, TILE)))


def ones_where(mask):
    return jnp.where(mask, 1.0, 0.0)


def group_and_rank(chain_row, axis):
    across = jnp.broadcast_to(chain_row, (TILE, TILE))
    down = jnp.transpose(across)
    group_across = jnp.floor(across * (1.0 / GROUP_TOKENS))
    group_down = jnp.floor(down * (1.0 / GROUP_TOKENS))
    same = group_across == group_down
    if axis == 0:
        rank = jnp.sum(ones_where(same & (down < across)), axis=0, keepdims=True)
        return group_across[0:1], rank
    rank = jnp.sum(ones_where(same & (across < down)), axis=1, keepdims=True)
    return group_down[:, 0:1], rank


def fused_kernel(
    sizes,
    query_hbm,
    key_hbm,
    value_hbm,
    grad_hbm,
    chain_ref,
    load_ref,
    length_ref,
    back_ref,
    roots_ref,
    rows_in,
    packed,
    landed,
    outgoing,
    load_own,
    load_all,
    spread,
    gathered,
    carry_low,
    onward_low,
    inside,
    inside_turned,
    root_wide,
    inner_wide,
    row_facts,
    queries,
    kept_queries,
    keys,
    kept_keys,
    values,
    kept_values,
    grads,
    dgrads,
    raw,
    extra_out,
    scores_turned,
    state_own,
    state_all,
    back_own,
    back_all,
    stage_one,
    stage_two,
    root_tile,
    root_sem,
    in_sem,
    load_sem,
    data_send,
    data_recv,
    state_send,
    state_recv,
    sum_send,
    sum_recv,
    out_send,
    out_recv,
):
    main, extra = sizes
    rows_all = 4 * (main + extra)
    main_slots = SOURCES * main
    slots = main_slots + SOURCES * extra
    tiles, parts = slots // TILE, slots // PART
    early, late = pl.ds(0, 3 * main + 4 * extra), pl.ds(3 * main + 4 * extra, main)
    place, x = lax.axis_index("ctx"), lax.axis_index("head")
    y, z, c = place // 16, lax.rem(place // 2, 8), lax.rem(place, 2)
    mine = y * 2 + c

    def wrapped(value, size):
        return jnp.where(value >= size, value - size, value)

    rows_y = [wrapped(y + n, 4) for n in range(4)]
    plane = []
    for j in range(8):
        cc = c if j % 2 == 0 else 1 - c
        plane.append((rows_y[j // 2] * 16 + cc, rows_y[j // 2] * 2 + cc))

    def at(j, zz):
        return plane[j][0] + 2 * zz, plane[j][1]

    def height(i):
        half = (i + 1) // 2
        return wrapped(z + jnp.where(lax.rem(i, 2) == 1, 4 - half, 4 + half), 8)

    def each_other(act):
        def level(i, carry):
            zz = height(i)
            for j in range(8):
                act(*at(j, zz), zz)
            return carry

        lax.fori_loop(0, 7, level, 0)
        for j in range(1, 8):
            act(*at(j, z), z)

    def remote(src, dst, send, recv, ctx, head):
        return pltpu.make_async_remote_copy(
            src_ref=src,
            dst_ref=dst,
            send_sem=send,
            recv_sem=recv,
            device_id=(ctx, head),
            device_id_type=MESH,
        )

    def settle(ref, sem):
        pltpu.make_async_copy(ref, ref, sem).wait()

    inputs = (query_hbm, key_hbm, value_hbm, grad_hbm)
    for a, source in enumerate(inputs):
        pltpu.make_async_copy(source, rows_in.at[pl.ds(a * TILE, TILE)], in_sem.at[a]).start()

    barrier = pltpu.get_barrier_semaphore()

    def greet(ctx, head, zz):
        pl.semaphore_signal(barrier, inc=1, device_id=(ctx, x), device_id_type=MESH)

    each_other(greet)
    for j in range(1, 4):
        pl.semaphore_signal(
            barrier, inc=1, device_id=(place, wrapped(x + j, 4)), device_id_type=MESH
        )

    group, rank = group_and_rank(chain_ref[...].astype(F32), 0)
    targets = []
    for a in range(4):
        main_row = (a * main if a < 3 else 3 * main + 4 * extra) + rank
        extra_row = 3 * main + a * extra + rank - main
        targets.append(group * rows_all + jnp.where(rank < main, main_row, extra_row))
    target = jnp.concatenate(targets, axis=1).astype(jnp.int32)
    load_own[...] = jnp.broadcast_to(load_ref[...], (8, TILE))
    for a, source in enumerate(inputs):
        pltpu.make_async_copy(source, rows_in.at[pl.ds(a * TILE, TILE)], in_sem.at[a]).wait()
    pl.semaphore_wait(barrier, 66)

    owner = place // 8
    for j in range(8):
        ctx, unused = at(j, owner)
        send = load_sem.at[1 if j == 0 else 0]
        if j == 0:

            @pl.when(owner == z)
            def _():
                pltpu.make_async_copy(
                    load_own, load_all.at[lax.rem(place, 8)], load_sem.at[2]
                ).start()

            @pl.when(owner != z)
            def _():
                remote(
                    load_own, load_all.at[lax.rem(place, 8)], send, load_sem.at[2], ctx, x
                ).start()
        else:
            remote(load_own, load_all.at[lax.rem(place, 8)], send, load_sem.at[2], ctx, x).start()

    row_number = iota((rows_all, 4 * TILE), 0)

    def send_rows(slot, ctx, rows, recv):
        remote(
            packed.at[slot, rows], landed.at[place, rows], data_send, data_recv.at[recv], ctx, x
        ).start()

    def keep_rows(slot, rows, recv):
        pltpu.make_async_copy(
            packed.at[slot, rows], landed.at[place, rows], data_recv.at[recv]
        ).start()

    def pack_group(i, carry):
        goal = height(i)
        pick = ones_where(row_number + goal * rows_all == target).astype(LOW)
        block = nn(pick, rows_in[...]).astype(LOW)
        for head in range(HEADS_HERE):
            packed[goal * 8 + head] = block[:, head * TILE : (head + 1) * TILE]
        for j in range(8):
            ctx, head = at(j, goal)
            if j == 0:

                @pl.when(i < 7)
                def _():
                    send_rows(goal * 8 + head, ctx, early, 0)

            else:
                send_rows(goal * 8 + head, ctx, early, 0)
        return carry

    lax.fori_loop(0, 8, pack_group, 0)
    keep_rows(z * 8 + mine, early, 0)
    keep_rows(z * 8 + mine, late, 1)

    def send_late(ctx, head, zz):
        send_rows(zz * 8 + head, ctx, late, 1)

    each_other(send_late)

    down, across = iota((TILE, TILE), 0), iota((TILE, TILE), 1)
    lengths = jnp.broadcast_to(length_ref[...].astype(F32), (TILE, TILE))
    ends_down = jnp.sum(jnp.where(across <= down, lengths, 0.0), axis=1, keepdims=True)
    ends = jnp.transpose(jnp.broadcast_to(ends_down, (TILE, TILE)))
    base = (z * GROUP_TOKENS).astype(F32)
    top = base + float(GROUP_TOKENS)

    def goes_on(last_tokens, first):
        start = jnp.max(
            jnp.where(ends[0:1] <= last_tokens - 1.0, ends[0:1], 0.0), axis=1, keepdims=True
        )
        return ones_where(start < first)

    if extra:
        number, other = iota((PART, PART), 0), iota((PART, PART), 1)
        array, rest = number // 64, lax.rem(number, 64)
        goal = (rest // 4) * 16 + array * 4 + lax.rem(rest, 4)
        gathered[...] = ones_where(goal == other).astype(LOW)
        source, rest = number // 16, lax.rem(number, 16)
        origin = (rest // 4) * 64 + source * 4 + lax.rem(rest, 4)
        spread[...] = ones_where(origin == other).astype(LOW)

    settle(load_all, load_sem.at[2])
    below = ones_where(across < down).astype(LOW)
    slot_number = iota((TILE, slots), 1).astype(F32)
    fact_row, fact_lane = iota((8, TILE), 0), iota((8, TILE), 1)
    seen = jnp.zeros((1, TILE), F32)
    facts = jnp.zeros((8, slots), F32)
    for j in range(8):
        source = (load_all[j, 0:1] // TILE).astype(F32)
        source_wide = turned(source)
        same = ones_where(source_wide == across.astype(F32))
        earlier = nn(below, same.astype(LOW)) + seen
        place_in = jnp.sum(same * earlier, axis=1, keepdims=True)
        seen = seen + jnp.sum(same, axis=0, keepdims=True)
        source_column = source_wide[:, 0:1]
        slot = jnp.where(
            place_in < main,
            source_column * main + place_in,
            main_slots + source_column * extra + place_in - main,
        )
        pick = ones_where(slot == slot_number).astype(LOW)
        told = jnp.where(
            fact_row == 0, j, jnp.where(fact_row == 1, fact_lane, jnp.where(fact_row == 2, 1, 0))
        )
        facts = facts + nn(told.astype(F32).astype(LOW), pick)
    position = jnp.where(facts[2:3] > 0.5, base + facts[0:1] * TILE + facts[1:2], -1.0)
    row_facts[0:1] = position
    for t in range(tiles):
        tile = slice(t * TILE, (t + 1) * TILE)
        where = turned(position[:, tile])
        start = jnp.max(jnp.where(ends <= where, ends, 0.0), axis=1, keepdims=True)
        end = jnp.min(jnp.where(ends > where, ends, float(TOKENS)), axis=1, keepdims=True)
        start_all = jnp.broadcast_to(start, (TILE, TILE))
        end_all = jnp.broadcast_to(end, (TILE, TILE))
        carry_low[tile] = ones_where((start_all < base) & (where >= 0.0)).astype(LOW)
        onward_low[tile] = ones_where((end_all > top) & (where >= 0.0)).astype(LOW)
        reached = (position <= where[:, 0:1]) & (position >= start)
        inside[tile] = ones_where(reached).astype(LOW)
        row_facts[1:2, tile] = jnp.transpose(start_all)[0:1]
    for t in range(tiles):
        tile = slice(t * TILE, (t + 1) * TILE)
        where = turned(position[:, tile])[:, 0:1]
        reaching = (where <= position) & (where >= row_facts[1:2])
        inside_turned[tile] = ones_where(reaching).astype(LOW)

    def part(i):
        return pl.ds(pl.multiple_of(i * PART, PART), PART)

    settle(landed.at[:, early], data_recv.at[0])
    for a, ref in enumerate((queries, keys, values)):
        ref[0:main_slots] = landed[:, a * main : (a + 1) * main].reshape(main_slots, TILE)
    if extra:
        held = landed[:, 3 * main : 3 * main + 4 * extra].reshape(1024, TILE)
        side = jnp.concatenate([held[n * PART : (n + 1) * PART] for n in range(4)], axis=1)
        sorted_rows = nn(gathered[...], side).astype(LOW)
        for n in range(4):
            for a, ref in enumerate((queries, keys, values, grads)):
                ref[main_slots + n * 64 : main_slots + (n + 1) * 64] = sorted_rows[
                    a * 64 : (a + 1) * 64, n * TILE : (n + 1) * TILE
                ]

    kept_keys[...] = keys[...] * onward_low[...]
    state_own[...] = tn(kept_keys[...], values[...]).astype(LOW)
    for n in (1, 2):
        ctx, unused = at(0, wrapped(z + n, 8))
        remote(
            state_own, state_all.at[n - 1], state_send.at[0], state_recv.at[n - 1], ctx, x
        ).start()
    kept_queries[...] = queries[...] * carry_low[...]
    kept_values[...] = values[...] * onward_low[...]

    def forward_part(i, carry):
        rows = part(i)
        low = nt(queries[rows], keys[...]).astype(LOW) * inside[rows]
        raw[rows] = nn(low, values[...])
        return carry

    lax.fori_loop(0, parts, forward_part, 0)
    settle(state_all.at[0], state_recv.at[0])
    settle(state_all.at[1], state_recv.at[1])
    before = goes_on(base, base - float(GROUP_TOKENS))
    state = state_all[0].astype(F32) + before * state_all[1].astype(F32)
    state_low = state.astype(LOW)

    def put(array, i, value):
        sources = PART // main
        if i < main_slots // PART:
            outgoing[i * sources : (i + 1) * sources, array * main : (array + 1) * main] = (
                value.reshape(sources, main, TILE)
            )
        else:
            extra_out[array * 256 : (array + 1) * 256] = value

    def send_back(rows):
        def one(ctx, head, zz):
            remote(
                outgoing.at[ctx, rows], back_ref.at[z, mine, rows], out_send, out_recv, ctx, x
            ).start()

        each_other(one)
        pltpu.make_async_copy(
            outgoing.at[place, rows], back_ref.at[z, mine, rows], out_recv
        ).start()

    for i in range(parts):
        rows = slice(i * PART, (i + 1) * PART)
        whole = raw[rows] + nn(kept_queries[rows], state_low)
        raw[rows] = whole
        put(0, i, whole.astype(LOW))

    def tile_sums(product):
        row = iota((16, TILE), 0)
        total = jnp.zeros((16, TILE), F32)
        ones = jnp.ones((16, TILE), LOW)
        for t in range(tiles):
            tile = product(slice(t * TILE, (t + 1) * TILE))
            high = tile.astype(LOW)
            rest = (tile - high.astype(F32)).astype(LOW)
            total = jnp.where(row == t, nt(ones, high) + nt(ones, rest), total)
        return total

    settle(landed.at[:, late], data_recv.at[1])
    grads[0:main_slots] = landed[:, late].reshape(main_slots, TILE)
    stage_one[mine, 0] = tile_sums(lambda tile: raw[tile] * raw[tile])
    stage_one[mine, 1] = tile_sums(lambda tile: raw[tile] * grads[tile].astype(F32))
    for j in range(1, 8):
        ctx, unused = at(j, z)
        own = stage_one.at[mine]
        remote(own, own, sum_send.at[0], sum_recv.at[0], ctx, x).start()

    send_back(pl.ds(0, main))

    def turned_part(i, carry):
        rows = part(i)
        scores_turned[rows] = nt(keys[rows], queries[...]).astype(LOW) * inside_turned[rows]
        return carry

    lax.fori_loop(0, parts, turned_part, 0)
    settle(stage_one.at[pl.ds(0, 7)], sum_recv.at[0])
    partial = stage_one[0]
    for j in range(1, 8):
        partial = partial + stage_one[j]
    stage_two[x] = partial
    for j in range(1, 4):
        own = stage_two.at[x]
        remote(own, own, sum_send.at[1], sum_recv.at[1], place, wrapped(x + j, 4)).start()
    settle(stage_two.at[pl.ds(0, 3)], sum_recv.at[1])
    total = (stage_two[0] + stage_two[1]) + (stage_two[2] + stage_two[3])
    inverse = 1.0 / jnp.sqrt(total[0] / FEATURES + epsilon)
    inner = total[1] * inverse / FEATURES
    root_tile[...] = inverse
    scale = inverse * inner
    for t in range(tiles):
        root_wide[t * TILE : (t + 1) * TILE] = turned(inverse[t : t + 1])
        inner_wide[t * TILE : (t + 1) * TILE] = turned(scale[t : t + 1])
    dgrads[...] = (
        (grads[...].astype(F32) - raw[...] * inner_wide[...]) * root_wide[...]
    ).astype(LOW)

    back_own[...] = tn(kept_queries[...], dgrads[...]).astype(LOW)
    for n in (1, 2):
        ctx, unused = at(0, wrapped(z + 8 - n, 8))
        remote(
            back_own, back_all.at[n - 1], state_send.at[1], state_recv.at[n + 1], ctx, x
        ).start()

    for j in range(8):
        ctx = wrapped(place // 8 + j, 8) * 8 + mine
        if j == 0:

            @pl.when(ctx == place)
            def _():
                pltpu.make_async_copy(root_tile, roots_ref.at[z], root_sem.at[2]).start()

            @pl.when(ctx != place)
            def _():
                remote(
                    root_tile, roots_ref.at[z], root_sem.at[1], root_sem.at[2], ctx, x
                ).start()
        else:
            remote(root_tile, roots_ref.at[z], root_sem.at[0], root_sem.at[2], ctx, x).start()

    for i in range(parts):
        rows = slice(i * PART, (i + 1) * PART)
        mixed = nt(dgrads[rows], values[...]).astype(LOW) * inside[rows]
        kept = dgrads[rows] * carry_low[rows]
        put(1, i, (nn(mixed, keys[...]) + nt(kept, state_low)).astype(LOW))
    send_back(pl.ds(main, main))

    settle(back_all.at[0], state_recv.at[2])
    settle(back_all.at[1], state_recv.at[3])
    after = goes_on(top + float(GROUP_TOKENS), top)
    back = back_all[0].astype(F32) + after * back_all[1].astype(F32)
    back_low = back.astype(LOW)
    for i in range(parts):
        rows = slice(i * PART, (i + 1) * PART)
        mixed = nt(values[rows], dgrads[...]).astype(LOW) * inside_turned[rows]
        put(2, i, (nn(mixed, queries[...]) + nt(kept_values[rows], back_low)).astype(LOW))
        value_part = nn(scores_turned[rows], dgrads[...]) + nn(kept_keys[rows], back_low)
        put(3, i, value_part.astype(LOW))
    if extra:
        held = extra_out[...]
        blocks = []
        for n in range(4):
            pieces = [held[a * 256 + n * 64 : a * 256 + (n + 1) * 64] for a in range(4)]
            blocks.append(jnp.concatenate(pieces, axis=0))
        extra_rows = nn(spread[...], jnp.concatenate(blocks, axis=1)).astype(LOW)
        for n in range(4):
            outgoing[n * 16 : (n + 1) * 16, 4 * main : rows_all] = extra_rows[
                :, n * TILE : (n + 1) * TILE
            ].reshape(16, 4 * extra, TILE)
    send_back(pl.ds(2 * main, 2 * main + 4 * extra))

    settle(load_all.at[pl.ds(0, 7)], load_sem.at[0])

    @pl.when(owner != z)
    def _():
        settle(load_own, load_sem.at[1])

    settle(packed.at[pl.ds(0, 63)], data_send)
    settle(state_all, state_send.at[0])
    settle(back_all, state_send.at[1])
    settle(stage_one.at[pl.ds(0, 7)], sum_send.at[0])
    settle(stage_two.at[pl.ds(0, 3)], sum_send.at[1])
    settle(roots_ref.at[pl.ds(0, 7)], root_sem.at[0])

    @pl.when(wrapped(place // 8, 8) * 8 + mine != place)
    def _():
        settle(root_tile, root_sem.at[1])

    settle(roots_ref, root_sem.at[2])
    settle(outgoing.at[pl.ds(0, 63)], out_send)
    settle(outgoing, out_recv)


def unpack_kernel(
    sizes,
    chain_hbm,
    back_hbm,
    roots_hbm,
    attended_hbm,
    query_hbm,
    key_hbm,
    value_hbm,
    chain_ref,
    roots_ref,
    back,
    out,
    pick,
    in_sem,
    out_sem,
):
    main, extra = sizes
    rows_all = 4 * (main + extra)
    outputs = (attended_hbm, query_hbm, key_hbm, value_hbm)
    pairs = [pl.ds(2 * n, 2) for n in range(HEADS_HERE // 2)]
    pltpu.make_async_copy(chain_hbm, chain_ref, in_sem.at[4]).start()
    pltpu.make_async_copy(roots_hbm, roots_ref, in_sem.at[5]).start()
    for n, pair in enumerate(pairs):
        pltpu.make_async_copy(back_hbm.at[:, pair], back.at[:, pair], in_sem.at[n]).start()
    place = lax.axis_index("ctx")
    pltpu.make_async_copy(chain_hbm, chain_ref, in_sem.at[4]).wait()
    group, rank = group_and_rank(chain_ref[...].astype(F32), 1)
    number = iota((TILE, GROUPS * rows_all), 1).astype(F32)
    for a in range(4):
        row = jnp.where(rank < main, a * main + rank, 4 * main + a * extra + rank - main)
        pick[a * TILE : (a + 1) * TILE] = ones_where(group * rows_all + row == number).astype(LOW)
    lane = iota((TILE, TILE), 1).astype(F32)
    kinds = [(place * main, rank, rank < main)]
    if extra:
        kinds.append((SOURCES * main + place * extra, rank - main, rank >= main))
    spot = jnp.zeros((TILE, TILE), F32)
    pltpu.make_async_copy(roots_hbm, roots_ref, in_sem.at[5]).wait()
    for first, at_slot, chosen in kinds:
        wanted = jnp.where(chosen, lax.rem(first, TILE).astype(F32) + at_slot, -1.0)
        rows = jnp.zeros((TILE, TILE), F32)
        for g in range(GROUPS):
            rows = jnp.where(group == g, roots_ref[g, pl.ds(first // TILE, 1)], rows)
        spot = spot + jnp.where(wanted == lane, rows, 0.0)
    factor = jnp.sum(spot, axis=1, keepdims=True)

    for n, pair in enumerate(pairs):
        pltpu.make_async_copy(back_hbm.at[:, pair], back.at[:, pair], in_sem.at[n]).wait()
        both = [back[:, 2 * n + k].reshape(GROUPS * rows_all, TILE) for k in range(2)]
        found = nn(pick[...], jnp.concatenate(both, axis=1))
        lanes = pl.ds(2 * n * TILE, 2 * TILE)
        for a, ref in enumerate(outputs):
            block = found[a * TILE : (a + 1) * TILE]
            out[a, :, lanes] = (block * factor if a == 0 else block).astype(LOW)
            pltpu.make_async_copy(out.at[a, :, lanes], ref.at[:, lanes], out_sem.at[a, n]).start()
    for n in range(HEADS_HERE // 2):
        lanes = pl.ds(2 * n * TILE, 2 * TILE)
        for a, ref in enumerate(outputs):
            pltpu.make_async_copy(out.at[a, :, lanes], ref.at[:, lanes], out_sem.at[a, n]).wait()


def layer(sizes, query_in, key_in, value_in, out_grad, chain_order, load_order, doc_lengths):
    main, extra = sizes
    rows_all, slots = 4 * (main + extra), SOURCES * (main + extra)
    chain_row = chain_order.reshape(1, TILE)
    whole = pl.BlockSpec(memory_space=pltpu.VMEM)
    anywhere = pl.BlockSpec(memory_space=pl.ANY)
    wide = pltpu.VMEM((slots, TILE), F32)
    low = pltpu.VMEM((slots, TILE), LOW)
    square = pltpu.VMEM((slots, slots), LOW)
    blocks = pltpu.VMEM((SOURCES, rows_all, TILE), LOW)
    dma = pltpu.SemaphoreType.DMA
    returned, roots = pl.pallas_call(
        functools.partial(fused_kernel, sizes),
        out_shape=(
            jax.ShapeDtypeStruct((GROUPS, HEADS_HERE, rows_all, TILE), LOW),
            jax.ShapeDtypeStruct((GROUPS, 16, TILE), F32),
        ),
        in_specs=[anywhere] * 4 + [whole] * 3,
        out_specs=(anywhere, anywhere),
        scratch_shapes=[
            pltpu.VMEM((4 * TILE, HEADS_HERE * TILE), LOW),
            blocks,
            blocks,
            blocks,
            pltpu.VMEM((8, TILE), jnp.int32),
            pltpu.VMEM((8, 8, TILE), jnp.int32),
            pltpu.VMEM((PART, PART), LOW),
            pltpu.VMEM((PART, PART), LOW),
            low,
            low,
            square,
            square,
            wide,
            wide,
            pltpu.VMEM((8, slots), F32),
            low,
            low,
            low,
            low,
            low,
            low,
            low,
            low,
            wide,
            pltpu.VMEM((1024, TILE), LOW),
            square,
            pltpu.VMEM((TILE, TILE), LOW),
            pltpu.VMEM((2, TILE, TILE), LOW),
            pltpu.VMEM((TILE, TILE), LOW),
            pltpu.VMEM((2, TILE, TILE), LOW),
            pltpu.VMEM((8, 2, 16, TILE), F32),
            pltpu.VMEM((4, 2, 16, TILE), F32),
            pltpu.VMEM((16, TILE), F32),
            dma((3,)),
            dma((4,)),
            dma((3,)),
            dma,
            dma((2,)),
            dma((2,)),
            dma((4,)),
            dma((2,)),
            dma((2,)),
            dma,
            dma,
        ],
        compiler_params=pltpu.CompilerParams(
            collective_id=1 if extra else 2, has_side_effects=True, vmem_limit_bytes=62 << 20
        ),
        name="fused",
    )(
        query_in,
        key_in,
        value_in,
        out_grad,
        chain_row,
        load_order.reshape(1, TILE),
        doc_lengths.reshape(1, TILE),
    )
    out = jax.ShapeDtypeStruct((TILE, HEADS_HERE * TILE), LOW)
    return pl.pallas_call(
        functools.partial(unpack_kernel, sizes),
        out_shape=(out,) * 4,
        in_specs=[anywhere] * 3,
        out_specs=(anywhere,) * 4,
        scratch_shapes=[
            pltpu.VMEM((1, TILE), jnp.int32),
            pltpu.VMEM((GROUPS, 16, TILE), F32),
            pltpu.VMEM((GROUPS, HEADS_HERE, rows_all, TILE), LOW),
            pltpu.VMEM((4, TILE, HEADS_HERE * TILE), LOW),
            pltpu.VMEM((4 * TILE, GROUPS * rows_all), LOW),
            dma((6,)),
            dma((4, 4)),
        ],
        compiler_params=pltpu.CompilerParams(vmem_limit_bytes=62 << 20),
        name="unpack",
    )(chain_row, returned, roots)


def most_kernel(chain_ref, most_ref):
    ahead = chain_ref[...] // TILE - lax.axis_index("ctx")
    ahead = jnp.where(ahead < 0, ahead + SOURCES, ahead)
    past = jnp.broadcast_to(ahead, (SOURCES, TILE)) - iota((SOURCES, TILE), 0)
    past = jnp.where(past < 0, past + SOURCES, past)
    counts = jnp.sum(ones_where(past < GROUPS), axis=1, keepdims=True)
    most_ref[0] = jnp.max(counts).astype(jnp.int32)


def body(query_in, key_in, value_in, out_grad, chain_order, load_order, doc_lengths):
    most = pl.pallas_call(
        most_kernel,
        out_shape=jax.ShapeDtypeStruct((1,), jnp.int32),
        in_specs=[pl.BlockSpec(memory_space=pltpu.VMEM)],
        out_specs=pl.BlockSpec(memory_space=pltpu.SMEM),
        name="most",
    )(chain_order.reshape(1, TILE))
    return lax.cond(
        most[0] <= sum(SMALL),
        functools.partial(layer, SMALL),
        functools.partial(layer, LARGE),
        query_in,
        key_in,
        value_in,
        out_grad,
        chain_order,
        load_order,
        doc_lengths,
    )


def solution(mesh):
    return jax.shard_map(
        body,
        mesh=mesh,
        in_specs=(
            P("ctx", "head"),
            P("ctx", "head"),
            P("ctx", "head"),
            P("ctx", "head"),
            P("ctx"),
            P("ctx"),
            P(),
        ),
        out_specs=(P("ctx", "head"), P("ctx", "head"), P("ctx", "head"), P("ctx", "head")),
        check_vma=False,
    )
```

```python
import functools
import jax
import jax.numpy as jnp
from jax import lax
from jax.experimental import pallas as pl
from jax.experimental.pallas import tpu as pltpu
from jax.sharding import PartitionSpec as P

HEAD_DIM = 128
FEATURES = 4096

epsilon = 1e-06

SOURCES = 64
GROUPS = 8
GROUP_TOKENS = 1024
TILE = 128
PART = 256
TOKENS = 8192
HEADS_HERE = 8
SMALL = (16, 4)
LARGE = (32, 0)
MESH = pl.DeviceIdType.MESH
F32 = jnp.float32
LOW = jnp.bfloat16


def nn(left, right, precision=None):
    return lax.dot_general(
        left, right, (((1,), (0,)), ((), ())), precision=precision, preferred_element_type=F32
    )


def nt(left, right, precision=None):
    return lax.dot_general(
        left, right, (((1,), (1,)), ((), ())), precision=precision, preferred_element_type=F32
    )


def tn(left, right):
    return lax.dot_general(left, right, (((0,), (0,)), ((), ())), preferred_element_type=F32)


def iota(shape, dim):
    return lax.broadcasted_iota(jnp.int32, shape, dim)


def turned(row):
    return jnp.transpose(jnp.broadcast_to(row, (TILE, TILE)))


def ones_where(mask):
    return jnp.where(mask, 1.0, 0.0)


def group_and_rank(chain_row, axis):
    across = jnp.broadcast_to(chain_row, (TILE, TILE))
    down = jnp.transpose(across)
    group_across = jnp.floor(across * (1.0 / GROUP_TOKENS))
    group_down = jnp.floor(down * (1.0 / GROUP_TOKENS))
    same = group_across == group_down
    if axis == 0:
        rank = jnp.sum(ones_where(same & (down < across)), axis=0, keepdims=True)
        return group_across[0:1], rank
    rank = jnp.sum(ones_where(same & (across < down)), axis=1, keepdims=True)
    return group_down[:, 0:1], rank


def fused_kernel(
    sizes,
    query_hbm,
    key_hbm,
    value_hbm,
    grad_hbm,
    chain_ref,
    load_ref,
    length_ref,
    back_ref,
    roots_ref,
    rows_in,
    packed,
    landed,
    outgoing,
    load_own,
    load_all,
    spread,
    gathered,
    carry_low,
    onward_low,
    inside,
    inside_turned,
    root_wide,
    inner_wide,
    row_facts,
    queries,
    kept_queries,
    keys,
    kept_keys,
    values,
    kept_values,
    grads,
    dgrads,
    raw,
    extra_out,
    scores_turned,
    state_own,
    state_all,
    back_own,
    back_all,
    stage_one,
    stage_two,
    root_tile,
    root_sem,
    in_sem,
    load_sem,
    data_send,
    data_recv,
    state_send,
    state_recv,
    sum_send,
    sum_recv,
    out_send,
    out_recv,
):
    main, extra = sizes
    rows_all = 4 * (main + extra)
    main_slots = SOURCES * main
    slots = main_slots + SOURCES * extra
    tiles, parts = slots // TILE, slots // PART
    early, late = pl.ds(0, 3 * main + 4 * extra), pl.ds(3 * main + 4 * extra, main)
    place, x = lax.axis_index("ctx"), lax.axis_index("head")
    y, z, c = place // 16, lax.rem(place // 2, 8), lax.rem(place, 2)
    mine = y * 2 + c

    def wrapped(value, size):
        return jnp.where(value >= size, value - size, value)

    rows_y = [wrapped(y + n, 4) for n in range(4)]
    plane = []
    for j in range(8):
        cc = c if j % 2 == 0 else 1 - c
        plane.append((rows_y[j // 2] * 16 + cc, rows_y[j // 2] * 2 + cc))

    def at(j, zz):
        return plane[j][0] + 2 * zz, plane[j][1]

    def height(i):
        half = (i + 1) // 2
        return wrapped(z + jnp.where(lax.rem(i, 2) == 1, 4 - half, 4 + half), 8)

    def each_other(act):
        def level(i, carry):
            zz = height(i)
            for j in range(8):
                act(*at(j, zz), zz)
            return carry

        lax.fori_loop(0, 7, level, 0)
        for j in range(1, 8):
            act(*at(j, z), z)

    def remote(src, dst, send, recv, ctx, head):
        return pltpu.make_async_remote_copy(
            src_ref=src,
            dst_ref=dst,
            send_sem=send,
            recv_sem=recv,
            device_id=(ctx, head),
            device_id_type=MESH,
        )

    def settle(ref, sem):
        pltpu.make_async_copy(ref, ref, sem).wait()

    inputs = (query_hbm, key_hbm, value_hbm, grad_hbm)
    for a, source in enumerate(inputs):
        pltpu.make_async_copy(source, rows_in.at[pl.ds(a * TILE, TILE)], in_sem.at[a]).start()

    barrier = pltpu.get_barrier_semaphore()

    def greet(ctx, head, zz):
        pl.semaphore_signal(barrier, inc=1, device_id=(ctx, x), device_id_type=MESH)

    each_other(greet)
    for j in range(1, 4):
        pl.semaphore_signal(
            barrier, inc=1, device_id=(place, wrapped(x + j, 4)), device_id_type=MESH
        )

    group, rank = group_and_rank(chain_ref[...].astype(F32), 0)
    targets = []
    for a in range(4):
        main_row = (a * main if a < 3 else 3 * main + 4 * extra) + rank
        extra_row = 3 * main + a * extra + rank - main
        targets.append(group * rows_all + jnp.where(rank < main, main_row, extra_row))
    target = jnp.concatenate(targets, axis=1).astype(jnp.int32)
    load_own[...] = jnp.broadcast_to(load_ref[...], (8, TILE))
    for a, source in enumerate(inputs):
        pltpu.make_async_copy(source, rows_in.at[pl.ds(a * TILE, TILE)], in_sem.at[a]).wait()
    pl.semaphore_wait(barrier, 66)

    owner = place // 8
    for j in range(8):
        ctx, unused = at(j, owner)
        send = load_sem.at[1 if j == 0 else 0]
        if j == 0:

            @pl.when(owner == z)
            def _():
                pltpu.make_async_copy(
                    load_own, load_all.at[lax.rem(place, 8)], load_sem.at[2]
                ).start()

            @pl.when(owner != z)
            def _():
                remote(
                    load_own, load_all.at[lax.rem(place, 8)], send, load_sem.at[2], ctx, x
                ).start()
        else:
            remote(load_own, load_all.at[lax.rem(place, 8)], send, load_sem.at[2], ctx, x).start()

    row_number = iota((rows_all, 4 * TILE), 0)

    def send_rows(slot, ctx, rows, recv):
        remote(
            packed.at[slot, rows], landed.at[place, rows], data_send, data_recv.at[recv], ctx, x
        ).start()

    def keep_rows(slot, rows, recv):
        pltpu.make_async_copy(
            packed.at[slot, rows], landed.at[place, rows], data_recv.at[recv]
        ).start()

    def pack_group(i, carry):
        goal = height(i)
        pick = ones_where(row_number + goal * rows_all == target).astype(LOW)
        block = nn(pick, rows_in[...]).astype(LOW)
        for head in range(HEADS_HERE):
            packed[goal * 8 + head] = block[:, head * TILE : (head + 1) * TILE]
        for j in range(8):
            ctx, head = at(j, goal)
            if j == 0:

                @pl.when(i < 7)
                def _():
                    send_rows(goal * 8 + head, ctx, early, 0)

            else:
                send_rows(goal * 8 + head, ctx, early, 0)
        return carry

    lax.fori_loop(0, 8, pack_group, 0)
    keep_rows(z * 8 + mine, early, 0)
    keep_rows(z * 8 + mine, late, 1)

    def send_late(ctx, head, zz):
        send_rows(zz * 8 + head, ctx, late, 1)

    each_other(send_late)

    down, across = iota((TILE, TILE), 0), iota((TILE, TILE), 1)
    lengths = jnp.broadcast_to(length_ref[...].astype(F32), (TILE, TILE))
    ends_down = jnp.sum(jnp.where(across <= down, lengths, 0.0), axis=1, keepdims=True)
    ends = jnp.transpose(jnp.broadcast_to(ends_down, (TILE, TILE)))
    base = (z * GROUP_TOKENS).astype(F32)
    top = base + float(GROUP_TOKENS)

    def goes_on(last_tokens, first):
        start = jnp.max(
            jnp.where(ends[0:1] <= last_tokens - 1.0, ends[0:1], 0.0), axis=1, keepdims=True
        )
        return ones_where(start < first)

    if extra:
        number, other = iota((PART, PART), 0), iota((PART, PART), 1)
        array, rest = number // 64, lax.rem(number, 64)
        goal = (rest // 4) * 16 + array * 4 + lax.rem(rest, 4)
        gathered[...] = ones_where(goal == other).astype(LOW)
        source, rest = number // 16, lax.rem(number, 16)
        origin = (rest // 4) * 64 + source * 4 + lax.rem(rest, 4)
        spread[...] = ones_where(origin == other).astype(LOW)

    settle(load_all, load_sem.at[2])
    below = ones_where(across < down).astype(LOW)
    slot_number = iota((TILE, slots), 1).astype(F32)
    fact_row, fact_lane = iota((8, TILE), 0), iota((8, TILE), 1)
    seen = jnp.zeros((1, TILE), F32)
    facts = jnp.zeros((8, slots), F32)
    for j in range(8):
        source = (load_all[j, 0:1] // TILE).astype(F32)
        source_wide = turned(source)
        same = ones_where(source_wide == across.astype(F32))
        earlier = nn(below, same.astype(LOW)) + seen
        place_in = jnp.sum(same * earlier, axis=1, keepdims=True)
        seen = seen + jnp.sum(same, axis=0, keepdims=True)
        source_column = source_wide[:, 0:1]
        slot = jnp.where(
            place_in < main,
            source_column * main + place_in,
            main_slots + source_column * extra + place_in - main,
        )
        pick = ones_where(slot == slot_number).astype(LOW)
        told = jnp.where(
            fact_row == 0, j, jnp.where(fact_row == 1, fact_lane, jnp.where(fact_row == 2, 1, 0))
        )
        facts = facts + nn(told.astype(F32).astype(LOW), pick)
    position = jnp.where(facts[2:3] > 0.5, base + facts[0:1] * TILE + facts[1:2], -1.0)
    row_facts[0:1] = position
    for t in range(tiles):
        tile = slice(t * TILE, (t + 1) * TILE)
        where = turned(position[:, tile])
        start = jnp.max(jnp.where(ends <= where, ends, 0.0), axis=1, keepdims=True)
        end = jnp.min(jnp.where(ends > where, ends, float(TOKENS)), axis=1, keepdims=True)
        start_all = jnp.broadcast_to(start, (TILE, TILE))
        end_all = jnp.broadcast_to(end, (TILE, TILE))
        carry_low[tile] = ones_where((start_all < base) & (where >= 0.0)).astype(LOW)
        onward_low[tile] = ones_where((end_all > top) & (where >= 0.0)).astype(LOW)
        reached = (position <= where[:, 0:1]) & (position >= start)
        inside[tile] = ones_where(reached).astype(LOW)
        row_facts[1:2, tile] = jnp.transpose(start_all)[0:1]
    for t in range(tiles):
        tile = slice(t * TILE, (t + 1) * TILE)
        where = turned(position[:, tile])[:, 0:1]
        reaching = (where <= position) & (where >= row_facts[1:2])
        inside_turned[tile] = ones_where(reaching).astype(LOW)

    def part(i):
        return pl.ds(pl.multiple_of(i * PART, PART), PART)

    settle(landed.at[:, early], data_recv.at[0])
    for a, ref in enumerate((queries, keys, values)):
        ref[0:main_slots] = landed[:, a * main : (a + 1) * main].reshape(main_slots, TILE)
    if extra:
        held = landed[:, 3 * main : 3 * main + 4 * extra].reshape(1024, TILE)
        side = jnp.concatenate([held[n * PART : (n + 1) * PART] for n in range(4)], axis=1)
        sorted_rows = nn(gathered[...], side).astype(LOW)
        for n in range(4):
            for a, ref in enumerate((queries, keys, values, grads)):
                ref[main_slots + n * 64 : main_slots + (n + 1) * 64] = sorted_rows[
                    a * 64 : (a + 1) * 64, n * TILE : (n + 1) * TILE
                ]

    kept_keys[...] = keys[...] * onward_low[...]
    state_own[...] = tn(kept_keys[...], values[...]).astype(LOW)
    for n in (1, 2):
        ctx, unused = at(0, wrapped(z + n, 8))
        remote(
            state_own, state_all.at[n - 1], state_send.at[0], state_recv.at[n - 1], ctx, x
        ).start()
    kept_queries[...] = queries[...] * carry_low[...]
    kept_values[...] = values[...] * onward_low[...]

    def forward_part(i, carry):
        rows = part(i)
        low = nt(queries[rows], keys[...]).astype(LOW) * inside[rows]
        raw[rows] = nn(low, values[...])
        return carry

    lax.fori_loop(0, parts, forward_part, 0)
    settle(state_all.at[0], state_recv.at[0])
    settle(state_all.at[1], state_recv.at[1])
    before = goes_on(base, base - float(GROUP_TOKENS))
    state = state_all[0].astype(F32) + before * state_all[1].astype(F32)
    state_low = state.astype(LOW)

    def put(array, i, value):
        sources = PART // main
        if i < main_slots // PART:
            outgoing[i * sources : (i + 1) * sources, array * main : (array + 1) * main] = (
                value.reshape(sources, main, TILE)
            )
        else:
            extra_out[array * 256 : (array + 1) * 256] = value

    def send_back(rows):
        def one(ctx, head, zz):
            remote(
                outgoing.at[ctx, rows], back_ref.at[z, mine, rows], out_send, out_recv, ctx, x
            ).start()

        each_other(one)
        pltpu.make_async_copy(
            outgoing.at[place, rows], back_ref.at[z, mine, rows], out_recv
        ).start()

    for i in range(parts):
        rows = slice(i * PART, (i + 1) * PART)
        whole = raw[rows] + nn(kept_queries[rows], state_low)
        raw[rows] = whole
        put(0, i, whole.astype(LOW))

    def tile_sums(product):
        row = iota((16, TILE), 0)
        total = jnp.zeros((16, TILE), F32)
        ones = jnp.ones((16, TILE), LOW)
        for t in range(tiles):
            tile = product(slice(t * TILE, (t + 1) * TILE))
            high = tile.astype(LOW)
            rest = (tile - high.astype(F32)).astype(LOW)
            total = jnp.where(row == t, nt(ones, high) + nt(ones, rest), total)
        return total

    settle(landed.at[:, late], data_recv.at[1])
    grads[0:main_slots] = landed[:, late].reshape(main_slots, TILE)
    stage_one[mine, 0] = tile_sums(lambda tile: raw[tile] * raw[tile])
    stage_one[mine, 1] = tile_sums(lambda tile: raw[tile] * grads[tile].astype(F32))
    for j in range(1, 8):
        ctx, unused = at(j, z)
        own = stage_one.at[mine]
        remote(own, own, sum_send.at[0], sum_recv.at[0], ctx, x).start()

    send_back(pl.ds(0, main))

    def turned_part(i, carry):
        rows = part(i)
        scores_turned[rows] = nt(keys[rows], queries[...]).astype(LOW) * inside_turned[rows]
        return carry

    lax.fori_loop(0, parts, turned_part, 0)
    settle(stage_one.at[pl.ds(0, 7)], sum_recv.at[0])
    partial = stage_one[0]
    for j in range(1, 8):
        partial = partial + stage_one[j]
    stage_two[x] = partial
    for j in range(1, 4):
        own = stage_two.at[x]
        remote(own, own, sum_send.at[1], sum_recv.at[1], place, wrapped(x + j, 4)).start()
    settle(stage_two.at[pl.ds(0, 3)], sum_recv.at[1])
    total = (stage_two[0] + stage_two[1]) + (stage_two[2] + stage_two[3])
    inverse = 1.0 / jnp.sqrt(total[0] / FEATURES + epsilon)
    inner = total[1] * inverse / FEATURES
    root_tile[...] = inverse
    scale = inverse * inner
    for t in range(tiles):
        root_wide[t * TILE : (t + 1) * TILE] = turned(inverse[t : t + 1])
        inner_wide[t * TILE : (t + 1) * TILE] = turned(scale[t : t + 1])
    dgrads[...] = (
        (grads[...].astype(F32) - raw[...] * inner_wide[...]) * root_wide[...]
    ).astype(LOW)

    back_own[...] = tn(kept_queries[...], dgrads[...]).astype(LOW)
    for n in (1, 2):
        ctx, unused = at(0, wrapped(z + 8 - n, 8))
        remote(
            back_own, back_all.at[n - 1], state_send.at[1], state_recv.at[n + 1], ctx, x
        ).start()

    for j in range(8):
        ctx = wrapped(place // 8 + j, 8) * 8 + mine
        if j == 0:

            @pl.when(ctx == place)
            def _():
                pltpu.make_async_copy(root_tile, roots_ref.at[z], root_sem.at[2]).start()

            @pl.when(ctx != place)
            def _():
                remote(
                    root_tile, roots_ref.at[z], root_sem.at[1], root_sem.at[2], ctx, x
                ).start()
        else:
            remote(root_tile, roots_ref.at[z], root_sem.at[0], root_sem.at[2], ctx, x).start()

    for i in range(parts):
        rows = slice(i * PART, (i + 1) * PART)
        mixed = nt(dgrads[rows], values[...]).astype(LOW) * inside[rows]
        kept = dgrads[rows] * carry_low[rows]
        put(1, i, (nn(mixed, keys[...]) + nt(kept, state_low)).astype(LOW))
    send_back(pl.ds(main, main))

    settle(back_all.at[0], state_recv.at[2])
    settle(back_all.at[1], state_recv.at[3])
    after = goes_on(top + float(GROUP_TOKENS), top)
    back = back_all[0].astype(F32) + after * back_all[1].astype(F32)
    back_low = back.astype(LOW)
    for i in range(parts):
        rows = slice(i * PART, (i + 1) * PART)
        mixed = nt(values[rows], dgrads[...]).astype(LOW) * inside_turned[rows]
        put(2, i, (nn(mixed, queries[...]) + nt(kept_values[rows], back_low)).astype(LOW))
    send_back(pl.ds(2 * main, main))
    for i in range(parts):
        rows = slice(i * PART, (i + 1) * PART)
        value_part = nn(scores_turned[rows], dgrads[...]) + nn(kept_keys[rows], back_low)
        put(3, i, value_part.astype(LOW))
    if extra:
        held = extra_out[...]
        blocks = []
        for n in range(4):
            pieces = [held[a * 256 + n * 64 : a * 256 + (n + 1) * 64] for a in range(4)]
            blocks.append(jnp.concatenate(pieces, axis=0))
        extra_rows = nn(spread[...], jnp.concatenate(blocks, axis=1)).astype(LOW)
        for n in range(4):
            outgoing[n * 16 : (n + 1) * 16, 4 * main : rows_all] = extra_rows[
                :, n * TILE : (n + 1) * TILE
            ].reshape(16, 4 * extra, TILE)
    send_back(pl.ds(3 * main, main + 4 * extra))

    settle(load_all.at[pl.ds(0, 7)], load_sem.at[0])

    @pl.when(owner != z)
    def _():
        settle(load_own, load_sem.at[1])

    settle(packed.at[pl.ds(0, 63)], data_send)
    settle(state_all, state_send.at[0])
    settle(back_all, state_send.at[1])
    settle(stage_one.at[pl.ds(0, 7)], sum_send.at[0])
    settle(stage_two.at[pl.ds(0, 3)], sum_send.at[1])
    settle(roots_ref.at[pl.ds(0, 7)], root_sem.at[0])

    @pl.when(wrapped(place // 8, 8) * 8 + mine != place)
    def _():
        settle(root_tile, root_sem.at[1])

    settle(roots_ref, root_sem.at[2])
    settle(outgoing.at[pl.ds(0, 63)], out_send)
    settle(outgoing, out_recv)


def unpack_kernel(
    sizes,
    chain_hbm,
    back_hbm,
    roots_hbm,
    attended_hbm,
    query_hbm,
    key_hbm,
    value_hbm,
    chain_ref,
    roots_ref,
    back,
    out,
    pick,
    in_sem,
    out_sem,
):
    main, extra = sizes
    rows_all = 4 * (main + extra)
    outputs = (attended_hbm, query_hbm, key_hbm, value_hbm)
    pairs = [pl.ds(2 * n, 2) for n in range(HEADS_HERE // 2)]
    pltpu.make_async_copy(chain_hbm, chain_ref, in_sem.at[4]).start()
    pltpu.make_async_copy(roots_hbm, roots_ref, in_sem.at[5]).start()
    for n, pair in enumerate(pairs):
        pltpu.make_async_copy(back_hbm.at[:, pair], back.at[:, pair], in_sem.at[n]).start()
    place = lax.axis_index("ctx")
    pltpu.make_async_copy(chain_hbm, chain_ref, in_sem.at[4]).wait()
    group, rank = group_and_rank(chain_ref[...].astype(F32), 1)
    number = iota((TILE, GROUPS * rows_all), 1).astype(F32)
    for a in range(4):
        row = jnp.where(rank < main, a * main + rank, 4 * main + a * extra + rank - main)
        pick[a * TILE : (a + 1) * TILE] = ones_where(group * rows_all + row == number).astype(LOW)
    lane = iota((TILE, TILE), 1).astype(F32)
    kinds = [(place * main, rank, rank < main)]
    if extra:
        kinds.append((SOURCES * main + place * extra, rank - main, rank >= main))
    spot = jnp.zeros((TILE, TILE), F32)
    pltpu.make_async_copy(roots_hbm, roots_ref, in_sem.at[5]).wait()
    for first, at_slot, chosen in kinds:
        wanted = jnp.where(chosen, lax.rem(first, TILE).astype(F32) + at_slot, -1.0)
        rows = jnp.zeros((TILE, TILE), F32)
        for g in range(GROUPS):
            rows = jnp.where(group == g, roots_ref[g, pl.ds(first // TILE, 1)], rows)
        spot = spot + jnp.where(wanted == lane, rows, 0.0)
    factor = jnp.sum(spot, axis=1, keepdims=True)

    for n, pair in enumerate(pairs):
        pltpu.make_async_copy(back_hbm.at[:, pair], back.at[:, pair], in_sem.at[n]).wait()
        both = [back[:, 2 * n + k].reshape(GROUPS * rows_all, TILE) for k in range(2)]
        found = nn(pick[...], jnp.concatenate(both, axis=1))
        lanes = pl.ds(2 * n * TILE, 2 * TILE)
        for a, ref in enumerate(outputs):
            block = found[a * TILE : (a + 1) * TILE]
            out[a, :, lanes] = (block * factor if a == 0 else block).astype(LOW)
            pltpu.make_async_copy(out.at[a, :, lanes], ref.at[:, lanes], out_sem.at[a, n]).start()
    for n in range(HEADS_HERE // 2):
        lanes = pl.ds(2 * n * TILE, 2 * TILE)
        for a, ref in enumerate(outputs):
            pltpu.make_async_copy(out.at[a, :, lanes], ref.at[:, lanes], out_sem.at[a, n]).wait()


def layer(sizes, query_in, key_in, value_in, out_grad, chain_order, load_order, doc_lengths):
    main, extra = sizes
    rows_all, slots = 4 * (main + extra), SOURCES * (main + extra)
    chain_row = chain_order.reshape(1, TILE)
    whole = pl.BlockSpec(memory_space=pltpu.VMEM)
    anywhere = pl.BlockSpec(memory_space=pl.ANY)
    wide = pltpu.VMEM((slots, TILE), F32)
    low = pltpu.VMEM((slots, TILE), LOW)
    square = pltpu.VMEM((slots, slots), LOW)
    blocks = pltpu.VMEM((SOURCES, rows_all, TILE), LOW)
    dma = pltpu.SemaphoreType.DMA
    returned, roots = pl.pallas_call(
        functools.partial(fused_kernel, sizes),
        out_shape=(
            jax.ShapeDtypeStruct((GROUPS, HEADS_HERE, rows_all, TILE), LOW),
            jax.ShapeDtypeStruct((GROUPS, 16, TILE), F32),
        ),
        in_specs=[anywhere] * 4 + [whole] * 3,
        out_specs=(anywhere, anywhere),
        scratch_shapes=[
            pltpu.VMEM((4 * TILE, HEADS_HERE * TILE), LOW),
            blocks,
            blocks,
            blocks,
            pltpu.VMEM((8, TILE), jnp.int32),
            pltpu.VMEM((8, 8, TILE), jnp.int32),
            pltpu.VMEM((PART, PART), LOW),
            pltpu.VMEM((PART, PART), LOW),
            low,
            low,
            square,
            square,
            wide,
            wide,
            pltpu.VMEM((8, slots), F32),
            low,
            low,
            low,
            low,
            low,
            low,
            low,
            low,
            wide,
            pltpu.VMEM((1024, TILE), LOW),
            square,
            pltpu.VMEM((TILE, TILE), LOW),
            pltpu.VMEM((2, TILE, TILE), LOW),
            pltpu.VMEM((TILE, TILE), LOW),
            pltpu.VMEM((2, TILE, TILE), LOW),
            pltpu.VMEM((8, 2, 16, TILE), F32),
            pltpu.VMEM((4, 2, 16, TILE), F32),
            pltpu.VMEM((16, TILE), F32),
            dma((3,)),
            dma((4,)),
            dma((3,)),
            dma,
            dma((2,)),
            dma((2,)),
            dma((4,)),
            dma((2,)),
            dma((2,)),
            dma,
            dma,
        ],
        compiler_params=pltpu.CompilerParams(
            collective_id=1 if extra else 2, has_side_effects=True, vmem_limit_bytes=62 << 20
        ),
        name="fused",
    )(
        query_in,
        key_in,
        value_in,
        out_grad,
        chain_row,
        load_order.reshape(1, TILE),
        doc_lengths.reshape(1, TILE),
    )
    out = jax.ShapeDtypeStruct((TILE, HEADS_HERE * TILE), LOW)
    return pl.pallas_call(
        functools.partial(unpack_kernel, sizes),
        out_shape=(out,) * 4,
        in_specs=[anywhere] * 3,
        out_specs=(anywhere,) * 4,
        scratch_shapes=[
            pltpu.VMEM((1, TILE), jnp.int32),
            pltpu.VMEM((GROUPS, 16, TILE), F32),
            pltpu.VMEM((GROUPS, HEADS_HERE, rows_all, TILE), LOW),
            pltpu.VMEM((4, TILE, HEADS_HERE * TILE), LOW),
            pltpu.VMEM((4 * TILE, GROUPS * rows_all), LOW),
            dma((6,)),
            dma((4, 4)),
        ],
        compiler_params=pltpu.CompilerParams(vmem_limit_bytes=62 << 20),
        name="unpack",
    )(chain_row, returned, roots)


def most_kernel(chain_ref, most_ref):
    ahead = chain_ref[...] // TILE - lax.axis_index("ctx")
    ahead = jnp.where(ahead < 0, ahead + SOURCES, ahead)
    past = jnp.broadcast_to(ahead, (SOURCES, TILE)) - iota((SOURCES, TILE), 0)
    past = jnp.where(past < 0, past + SOURCES, past)
    counts = jnp.sum(ones_where(past < GROUPS), axis=1, keepdims=True)
    most_ref[0] = jnp.max(counts).astype(jnp.int32)


def body(query_in, key_in, value_in, out_grad, chain_order, load_order, doc_lengths):
    most = pl.pallas_call(
        most_kernel,
        out_shape=jax.ShapeDtypeStruct((1,), jnp.int32),
        in_specs=[pl.BlockSpec(memory_space=pltpu.VMEM)],
        out_specs=pl.BlockSpec(memory_space=pltpu.SMEM),
        name="most",
    )(chain_order.reshape(1, TILE))
    return lax.cond(
        most[0] <= sum(SMALL),
        functools.partial(layer, SMALL),
        functools.partial(layer, LARGE),
        query_in,
        key_in,
        value_in,
        out_grad,
        chain_order,
        load_order,
        doc_lengths,
    )


def solution(mesh):
    return jax.shard_map(
        body,
        mesh=mesh,
        in_specs=(
            P("ctx", "head"),
            P("ctx", "head"),
            P("ctx", "head"),
            P("ctx", "head"),
            P("ctx"),
            P("ctx"),
            P(),
        ),
        out_specs=(P("ctx", "head"), P("ctx", "head"), P("ctx", "head"), P("ctx", "head")),
        check_vma=False,
    )
```
